128 devices in a mesh: prow: 8 (over y, x_hi), pcol: 16 (over z, x_lo, core).
Axes of the slice: x: 4 (x_hi: 2, x_lo: 2; x = x_hi * 2 + x_lo), y: 4, z: 4, core: 2. Of those that a mesh axis runs over, the one named last changes fastest.
Arguments:
- root_sigma: float32 [12288, 12288], P('prow', 'pcol')
- pivot_diag: float32 [128, 2, 3072], P(None, None, 'prow'), may hold values from -6 to 6
- update_l: float32 [3072, 12288], P('prow', 'pcol'), may hold values from -0.078125 to 0.078125
- update_map: int32 [2, 48], replicated, may hold values from 0 to 95, as said below
Outputs:
- pivot_update: float32 [3072, 12288], P('prow', 'pcol')
- marginal_cov: float32 [128, 2, 3072], P(None, None, 'prow')
The draws below stay inside these ranges and needn't reach their ends.
Inputs may be any that keep to these rules, and one draw needn't show every extreme that they name: `update_map`: for every child c and block i < 8, the entries r from i * 6 to (i + 1) * 6 - 1 are distinct, increasing, and all equal to i modulo 8.
All inputs are finite; a program needn't handle non-finite values.
Results may differ from the reference program's by a relative error of at most 0.0001.
Values sent between devices are 32-bit elements; how exact they have to be, the bound alone decides.
A program may use at most 128 MiB of HBM per device.

```python
import jax
import jax.numpy as jnp
from jax import lax

TILE = 128
ROOT = 12288
UPD = 6144
PIV = 3072
N_PROW = 8
N_PCOL = 16


def storage_order(groups):
    spots = jnp.arange(ROOT, dtype=jnp.int32)
    share = ROOT // groups
    tile_ids = spots // share + groups * (spots % share // TILE)
    return (tile_ids * TILE + spots % TILE).astype(jnp.int32)


def draw_root_sigma(key, part):
    key = jax.random.fold_in(key, 11)
    base = jax.random.normal(key, (ROOT, ROOT), jnp.float32)
    symmetric = (base + base.T) * 0.5
    rows_first = jnp.take(symmetric, storage_order(N_PROW), axis=0)
    return jnp.take(rows_first, storage_order(N_PCOL), axis=1)


def draw_update_map(key, part):
    key = jax.random.fold_in(key, 23)
    per_block = UPD // (TILE * N_PROW)
    stored_tiles = ROOT // (TILE * N_PROW)
    key_list = jax.random.split(key, 2 * N_PROW)
    row_ids = jnp.arange(2 * N_PROW, dtype=jnp.int32)
    targets = jnp.where(row_ids == 0, 0, jnp.where(row_ids == N_PROW - 1, stored_tiles - 1, -1)).astype(jnp.int32)

    def shuffled(subkey, target):
        order = jax.random.permutation(subkey, stored_tiles).astype(jnp.int32)
        first = order[0]
        swapped = jnp.where(order == target, first, order)
        swapped = swapped.at[0].set(target)
        return jnp.where(target >= 0, swapped, order)
    orders = jax.vmap(shuffled)(key_list, targets)[:, :per_block]
    chosen = jnp.sort(orders, axis=1).reshape(2, N_PROW, per_block)
    classes = jnp.arange(N_PROW, dtype=jnp.int32)[None, :, None]
    return (classes + N_PROW * chosen).astype(jnp.int32).reshape(2, UPD // TILE)


def shard_levels(own_key, extent, cuts, smallest, largest):
    factor_of = 1.0
    for axis_at, shards_of in cuts:
        draws = jax.random.uniform(jax.random.fold_in(jax.random.fold_in(own_key, 6), axis_at), (shards_of,), jnp.float32, smallest / len(cuts), largest / len(cuts))
        factor_of = factor_of * jnp.repeat(jnp.exp(draws), extent[axis_at] // shards_of).reshape((-1,) + (1,) * (len(extent) - 1 - axis_at))
    return factor_of


def scatter_about(rng, dims, deviation, limit, cuts=(), kind=jnp.bfloat16):
    entries = jax.random.normal(rng, dims, jnp.float32) * deviation
    if len(cuts) > 0:
        entries = shard_levels(rng, dims, cuts, -0.22, 0.18) * entries
    return jnp.clip(entries, min=-limit, max=limit).astype(kind)


def setup_inputs(seed: int = 0) -> dict:
    streams_of = jax.random.split(jax.random.key(seed), 5)
    root_sigma = draw_root_sigma(jax.random.fold_in(streams_of[4], 71), 0)
    pivot_diag = scatter_about(streams_of[1], (TILE, 2, PIV), 1.0, 6.0, ((2, 8),), jnp.float32)
    update_l = scatter_about(streams_of[2], (PIV, 2 * UPD), UPD ** -0.5, 0.078125, ((0, 8), (1, 16)), jnp.float32)
    update_map = draw_update_map(jax.random.fold_in(streams_of[4], 71), 0)
    return {"root_sigma": root_sigma, "pivot_diag": pivot_diag, "update_l": update_l, "update_map": update_map}


exact_mode = lax.Precision.HIGHEST


def stored_index(tile_ids, groups, per_group):
    spots = (tile_ids % groups) * per_group + tile_ids // groups
    inner = jnp.arange(TILE, dtype=jnp.int32)
    return (spots[:, None] * TILE + inner[None, :]).reshape(-1).astype(jnp.int32)


def reference(root_sigma, pivot_diag, update_l, update_map):
    row_tiles = ROOT // (TILE * N_PROW)
    col_tiles = ROOT // (TILE * N_PCOL)
    updates = []
    margins = []
    for child in range(2):
        tile_ids = update_map[child]
        row_index = stored_index(tile_ids, N_PROW, row_tiles)
        col_index = stored_index(tile_ids, N_PCOL, col_tiles)
        sigma_update = jnp.take(jnp.take(root_sigma, row_index, axis=0), col_index, axis=1)
        factor = update_l[:, child * UPD:(child + 1) * UPD]
        product = -jnp.dot(factor, sigma_update, precision=exact_mode, preferred_element_type=jnp.float32)
        updates.append(product)
        left = product.reshape(PIV // TILE, TILE, UPD)
        right = factor.reshape(PIV // TILE, TILE, UPD)
        tiles_diag = jnp.einsum("qrk,qsk->rqs", left, right, precision=exact_mode).reshape(TILE, PIV)
        margins.append(pivot_diag[:, child, :] - tiles_diag)
    pivot_update = jnp.concatenate(updates, axis=1)
    marginal_cov = jnp.stack(margins, axis=1)
    return pivot_update, marginal_cov
```

```python
import jax
import jax.numpy as jnp
from jax import lax
from jax.experimental import pallas as pl
from jax.experimental.pallas import tpu as pltpu
from jax.sharding import PartitionSpec as P

MESH = pl.DeviceIdType.MESH
F32, BF16 = jnp.float32, jnp.bfloat16
NT = (((1,), (1,)), ((), ()))


def split(x):
    hi = x.astype(BF16)
    return hi, (x - hi.astype(F32)).astype(BF16)


def kernel(umap, sig, pd, l_ref, c_out, m_out, fs, rc, stf, bhi, blo, lb, ahi, alo, prod, xr, zr, tr, dsend, dr, g,
           zs_s, zs_r, cs_s, cs_r, ls_s, l_r, fw_s, x_s, x_r, z_s, z_r, t_s, t_r, d_s, d_r, g_s, g_r):
    me_r, me_c = lax.axis_index("prow"), lax.axis_index("pcol")
    y, xh = me_r // 2, me_r % 2
    half, j = me_c // 8, me_c % 8
    zl, xl, k = j // 4, (j // 2) % 2, j % 2
    chunks = fs.shape[0]
    width = fs.shape[1]
    tile = sig.shape[1]
    tiles = 2 * chunks

    def dev(y_, xh_, zl_, xl_, k_):
        return (y_ * 2 + xh_, half * 8 + zl_ * 4 + xl_ * 2 + k_)

    partner = (me_r, (me_c + 8) % 16)
    other_core = dev(y, xh, zl, xl, 1 - k)
    x_peer = dev(y, xh, zl, 1 - xl, k)
    z_peer = dev(y, xh, 1 - zl, xl, k)
    y_final = 2 * zl + 1 - xl
    deliver = (y_final * 2 + (xh + k) % 2, half * 8 + me_r)
    source = ((2 * zl + xl) * 2 + k, half * 8 + (y // 2) * 4 + (1 - y % 2) * 2 + (xh + k) % 2)

    def copy(src, dst, ssem, rsem, to):
        return pltpu.make_async_remote_copy(
            src_ref=src, dst_ref=dst, send_sem=ssem, recv_sem=rsem, device_id=to, device_id_type=MESH)

    barrier = pltpu.get_barrier_semaphore()

    def greet(to):
        pl.semaphore_signal(barrier, inc=1, device_id=to, device_id_type=MESH)

    for d in range(1, 16):
        greet((me_r, (me_c + d) % 16))
    for d in range(1, 4):
        for kk in range(2):
            greet(dev((y + d) % 4, xh, zl, xl, kk))
    for kk in range(2):
        greet(dev(y, 1 - xh, zl, xl, kk))
    greet(source)
    pl.semaphore_wait(barrier, 24)

    def far_copy(q):
        return copy(fs.at[q], rc.at[q], zs_s.at[q], zs_r.at[q], partner)

    for q in range(chunks):
        for h in range(2):
            row = umap[1 - half, me_r * tiles + 2 * q + h] // 8
            fs[q, h * tile:(h + 1) * tile, :] = sig[row]
        far_copy(q).start()

    own_l = [copy(l_ref, lb.at[y, k], ls_s.at[d - 1], l_r.at[y, k], dev((y + d) % 4, xh, zl, xl, 0)) for d in range(1, 4)]
    own_l.append(copy(l_ref, lb.at[y, k], ls_s.at[3], l_r.at[y, k], dev(y, 1 - xh, zl, xl, 1)))
    own_l[3].start()
    for c in own_l[:3]:
        c.start()
    near_l = copy(l_ref, lb.at[y, k], ls_s.at[4], l_r.at[y, k], other_core)
    stay_l = pltpu.make_async_copy(l_ref, lb.at[y, 0], l_r.at[y, 0])

    @pl.when(k == 1)
    def _():
        near_l.start()

    @pl.when(k == 0)
    def _():
        stay_l.start()

    def forward(kk, d):
        return copy(lb.at[y, kk], lb.at[y, kk], fw_s.at[kk, d - 1], l_r.at[y, kk], dev((y + d) % 4, xh, zl, xl, 1))

    def core_copy(q):
        return copy(stf.at[k, q], stf.at[k, q], cs_s.at[q], cs_r.at[q], other_core)

    def take_s(q):
        far_copy(q).wait_recv()
        for h in range(2):
            row = umap[half, me_r * tiles + 2 * q + h] // 8
            near = sig[row]
            far = rc[q, h * tile:(h + 1) * tile, :]
            for s in range(tiles):
                col = umap[half, j * tiles + s]
                spot = col // 16 + tiles * (((col // 8) % 2 + half) % 2)
                x = near[:, :tile]
                for c in range(1, 2 * tiles):
                    lanes = slice((c % tiles) * tile, (c % tiles + 1) * tile)
                    x = jnp.where(spot == c, (near if c < tiles else far)[:, lanes], x)
                stf[k, q, s * tile:(s + 1) * tile, h * tile:(h + 1) * tile] = x.T
        core_copy(q).start()
        hi, lo = split(stf[k, q])
        bhi[q, k] = hi
        blo[q, k] = lo
        copy(stf.at[1 - k, q], stf.at[1 - k, q], cs_s.at[q], cs_r.at[q], other_core).wait_recv()
        hi, lo = split(stf[1 - k, q])
        bhi[q, 1 - k] = hi
        blo[q, 1 - k] = lo

    def x_copy(b, q):
        return copy(prod.at[xl + 2 * b, q], xr.at[b, q], x_s.at[b, q], x_r.at[b, q], x_peer)

    def slot(t, carry):
        yp = (y + t + (t // 2) * (1 - 2 * (t % 2))) % 4
        for kk in range(2):
            copy(lb.at[yp, kk], lb.at[yp, kk], ls_s.at[0], l_r.at[yp, kk], other_core).wait_recv()

        @pl.when((t == 0) & (k == 1))
        def _():
            for d in (1, 3, 2):
                for kk in range(2):
                    forward(kk, d).start()

        for kk in range(2):
            hi, lo = split(lb[yp, kk])
            ahi[kk] = hi
            alo[kk] = lo
        for q in range(chunks):
            @pl.when(t == 0)
            def _():
                take_s(q)

            total = jnp.zeros((ahi.shape[1], width), F32)
            for kk in range(2):
                total += jnp.dot(ahi[kk], bhi[q, kk], preferred_element_type=F32)
                total += jnp.dot(ahi[kk], blo[q, kk], preferred_element_type=F32)
                total += jnp.dot(alo[kk], bhi[q, kk], preferred_element_type=F32)
            prod[yp, q] = total

            @pl.when(yp % 2 == xl)
            def _():
                x_copy(yp // 2, q).start()
        return carry

    lax.fori_loop(0, 4, slot, 0)

    y_sent = 2 * (1 - zl) + 1 - xl

    def z_copy(q):
        return copy(prod.at[y_sent, q], zr.at[q], z_s.at[q], z_r.at[q], z_peer)

    def t_copy(q):
        return copy(prod.at[y_final, q], tr.at[q], t_s.at[q], t_r.at[q], deliver)

    for q in range(chunks):
        x_copy(1 - zl, q).wait_recv()
        prod[y_sent, q] = prod[y_sent, q] + xr[1 - zl, q]
        z_copy(q).start()
    for q in range(chunks):
        x_copy(zl, q).wait_recv()
        z_copy(q).wait_recv()
        prod[y_final, q] = -(prod[y_final, q] + xr[zl, q] + zr[q])
        t_copy(q).start()

    diag = [jnp.zeros((tile, tile), F32) for _ in range(l_ref.shape[0] // tile)]
    for q in range(chunks):
        t_copy(q).wait_recv()
        cols = slice(q * width, (q + 1) * width)
        c_out[:, cols] = tr[q]
        for t in range(len(diag)):
            rows = slice(t * tile, (t + 1) * tile)
            diag[t] += lax.dot_general(tr[q, rows], l_ref[rows, cols], NT, precision=lax.Precision.HIGHEST,
                                       preferred_element_type=F32)
    for t in range(len(diag)):
        dsend[:, :, t * tile:(t + 1) * tile] = diag[t].reshape(8, tile // 8, tile)

    def d_copy(d):
        to = (j + d) % 8
        return copy(dsend.at[to], dr.at[j], d_s.at[d], d_r.at[j], (me_r, half * 8 + to))

    def d_from(d):
        frm = (j + d) % 8
        return copy(dsend.at[frm], dr.at[frm], d_s.at[d], d_r.at[frm], (me_r, half * 8 + frm))

    for d in range(1, 8):
        d_copy(d).start()
    dr[j] = dsend[j]
    for d in range(1, 8):
        d_from(d).wait_recv()
    total = dr[0]
    for d in range(1, 8):
        total += dr[d]
    g[me_c] = total

    def g_copy(d):
        return copy(g.at[me_c], g.at[me_c], g_s.at[d], g_r.at[me_c], (me_r, (me_c + d) % 16))

    def g_from(d):
        frm = (me_c + d) % 16
        return copy(g.at[frm], g.at[frm], g_s.at[d], g_r.at[frm], (me_r, frm))

    for d in range(1, 16):
        g_copy(d).start()
    for d in range(1, 16):
        g_from(d).wait_recv()
    for h in range(2):
        m_out[:, h, :] = pd[:, h, :] - g[h * 8:(h + 1) * 8].reshape(tile, -1)

    for q in range(chunks):
        far_copy(q).wait_send()
        core_copy(q).wait_send()
        z_copy(q).wait_send()
        t_copy(q).wait_send()
        for b in range(2):
            x_copy(b, q).wait_send()
    for c in own_l:
        c.wait_send()

    @pl.when(k == 1)
    def _():
        near_l.wait_send()
        for d in range(1, 4):
            for kk in range(2):
                forward(kk, d).wait_send()

    for d in range(1, 8):
        d_copy(d).wait_send()
    for d in range(1, 16):
        g_copy(d).wait_send()


def local(root_sigma, pivot_diag, update_l, update_map):
    tile = pivot_diag.shape[0]
    rows, cols = update_l.shape
    chunks = 3
    width = cols // chunks
    sem = pltpu.SemaphoreType.DMA
    vmem = pl.BlockSpec(memory_space=pltpu.VMEM)
    return pl.pallas_call(
        kernel,
        out_shape=(jax.ShapeDtypeStruct(update_l.shape, F32), jax.ShapeDtypeStruct(pivot_diag.shape, F32)),
        in_specs=[pl.BlockSpec(memory_space=pltpu.SMEM), vmem, vmem, vmem],
        out_specs=(vmem, vmem),
        scratch_shapes=[
            pltpu.VMEM((chunks, width, cols), F32),
            pltpu.VMEM((chunks, width, cols), F32),
            pltpu.VMEM((2, chunks, cols, width), F32),
            pltpu.VMEM((chunks, 2, cols, width), BF16),
            pltpu.VMEM((chunks, 2, cols, width), BF16),
            pltpu.VMEM((4, 2, rows, cols), F32),
            pltpu.VMEM((2, rows, cols), BF16),
            pltpu.VMEM((2, rows, cols), BF16),
            pltpu.VMEM((4, chunks, rows, width), F32),
            pltpu.VMEM((2, chunks, rows, width), F32),
            pltpu.VMEM((chunks, rows, width), F32),
            pltpu.VMEM((chunks, rows, width), F32),
            pltpu.VMEM((8, tile // 8, rows), F32),
            pltpu.VMEM((8, tile // 8, rows), F32),
            pltpu.VMEM((16, tile // 8, rows), F32),
            sem((chunks,)), sem((chunks,)), sem((chunks,)), sem((chunks,)),
            sem((5,)), sem((4, 2)), sem((2, 3)),
            sem((2, chunks)), sem((2, chunks)), sem((chunks,)), sem((chunks,)), sem((chunks,)), sem((chunks,)),
            sem((8,)), sem((8,)), sem((16,)), sem((16,)),
        ],
        compiler_params=pltpu.CompilerParams(
            collective_id=0, has_side_effects=True, vmem_limit_bytes=60 * 2**20),
        name="selected_inverse",
    )(update_map, root_sigma.reshape(-1, tile, root_sigma.shape[1]), pivot_diag, update_l)


def solution(mesh):
    placed = (P("prow", "pcol"), P(None, None, "prow"), P("prow", "pcol"), P())
    return jax.shard_map(
        local,
        mesh=mesh,
        in_specs=placed,
        out_specs=(P("prow", "pcol"), P(None, None, "prow")),
        check_vma=False,
    )
```

```python
import jax
import jax.numpy as jnp
from jax import lax
from jax.experimental import pallas as pl
from jax.experimental.pallas import tpu as pltpu
from jax.sharding import PartitionSpec as P

MESH = pl.DeviceIdType.MESH
F32, BF16 = jnp.float32, jnp.bfloat16
NT = (((1,), (1,)), ((), ()))


def split(x):
    hi = x.astype(BF16)
    return hi, (x - hi.astype(F32)).astype(BF16)


def kernel(umap, sig, pd, l_ref, c_out, m_out, fs, rc, stf, bhi, blo, lx, lb, ahi, alo, prod, xr, zr, fin, leg, got, dsend, dr, g,
           zs_s, zs_r, cs_s, cs_r, lx_s, lx_r, l_s, f_s, l_r, x_s, x_r, z_s, z_r, a_s, a_r, b_s, b_r, d_s, d_r, g_s, g_r):
    me_r, me_c = lax.axis_index("prow"), lax.axis_index("pcol")
    y, xh = me_r // 2, me_r % 2
    half, j = me_c // 8, me_c % 8
    zl, xl, k = j // 4, (j // 2) % 2, j % 2
    chunks, width = fs.shape[0], fs.shape[1]
    tile = sig.shape[1]
    tiles = 2 * chunks
    rows = l_ref.shape[0]
    part = rows // 4
    steps = 4 * chunks

    def dev(y_, xh_, zl_, xl_, k_):
        return (y_ * 2 + xh_, half * 8 + zl_ * 4 + xl_ * 2 + k_)

    partner = (me_r, (me_c + 8) % 16)
    other_core = dev(y, xh, zl, xl, 1 - k)
    x_peer = dev(y, xh, zl, 1 - xl, k)
    z_peer = dev(y, xh, 1 - zl, xl, k)

    def copy(src, dst, ssem, rsem, to):
        return pltpu.make_async_remote_copy(
            src_ref=src, dst_ref=dst, send_sem=ssem, recv_sem=rsem, device_id=to, device_id_type=MESH)

    barrier = pltpu.get_barrier_semaphore()

    def greet(to):
        pl.semaphore_signal(barrier, inc=1, device_id=to, device_id_type=MESH)

    for d in range(1, 16):
        greet((me_r, (me_c + d) % 16))
    for d in range(4):
        greet(dev((y + d) % 4, 1 - xh, zl, xl, k))
        if d > 0:
            for kk in range(2):
                greet(dev((y + d) % 4, xh, zl, xl, kk))
    pl.semaphore_wait(barrier, 25)

    def cross():
        return copy(l_ref, lx, lx_s, lx_r, dev(y, 1 - xh, zl, xl, k))

    def spread(src, core, sems, d):
        return copy(src, lb.at[y, k], sems.at[d], l_r.at[y, k], dev((y + d) % 4, xh, zl, xl, core))

    def spread_start(src, core, sems):
        for d in (1, 3, 2):
            spread(src, core, sems, d).start()

        @pl.when(k != core)
        def _():
            spread(src, core, sems, 0).start()

        @pl.when(k == core)
        def _():
            pltpu.make_async_copy(src, lb.at[y, core], l_r.at[y, core]).start()

    def spread_end(src, core, sems):
        for d in (1, 3, 2):
            spread(src, core, sems, d).wait_send()

        @pl.when(k != core)
        def _():
            spread(src, core, sems, 0).wait_send()

    cross().start()

    def far_copy(q):
        return copy(fs.at[q], rc.at[q], zs_s.at[q], zs_r.at[q], partner)

    for q in range(chunks):
        for h in range(2):
            row = umap[1 - half, me_r * tiles + 2 * q + h] // 8
            fs[q, h * tile:(h + 1) * tile, :] = sig[row]
        far_copy(q).start()

    spread_start(l_ref, 0, l_s)

    def core_copy(kk, q):
        return copy(stf.at[kk, q], stf.at[kk, q], cs_s.at[q], cs_r.at[q], other_core)

    def take_s(q):
        far_copy(q).wait_recv()
        for h in range(2):
            row = umap[half, me_r * tiles + 2 * q + h] // 8
            near = sig[row]
            far = rc[q, h * tile:(h + 1) * tile, :]
            for s in range(tiles):
                col = umap[half, j * tiles + s]
                spot = col // 16 + tiles * (((col // 8) % 2 + half) % 2)
                x = near[:, :tile]
                for c in range(1, 2 * tiles):
                    lanes = slice((c % tiles) * tile, (c % tiles + 1) * tile)
                    x = jnp.where(spot == c, (near if c < tiles else far)[:, lanes], x)
                stf[k, q, s * tile:(s + 1) * tile, h * tile:(h + 1) * tile] = x.T
        core_copy(k, q).start()
        hi, lo = split(stf[k, q])
        bhi[q, k] = hi
        blo[q, k] = lo
        core_copy(1 - k, q).wait_recv()
        hi, lo = split(stf[1 - k, q])
        bhi[q, 1 - k] = hi
        blo[q, 1 - k] = lo

    def where_of(n):
        last = n // (3 * chunks)
        t = (1 - k) * ((1 - last) * (n % 3) + last * 3) + k * (n // chunks)
        q = (1 - k) * ((1 - last) * (n // 3) + last * (n - 3 * chunks)) + k * (n % chunks)
        return t, q, t + (t // 2) * (1 - 2 * (t % 2))

    def x_copy(t, q):
        return copy(prod.at[t, q, pl.ds(2 * part * (1 - xl), 2 * part)], xr.at[t, q], x_s.at[t, q], x_r.at[t, q], x_peer)

    def z_copy(t, q):
        return copy(xr.at[t, q, pl.ds(part * (1 - zl), part)], zr.at[t, q], z_s.at[t, q], z_r.at[t, q], z_peer)

    def a_copy(t, q, dy):
        return copy(fin.at[t, q], leg.at[y, q], a_s.at[t, q], a_r.at[y, q], dev((y + dy) % 4, (xh + k) % 2, zl, xl, k))

    spot_b = pl.ds(2 * part * xl + part * zl, part)

    def b_copy(ys, q):
        return copy(leg.at[ys, q], got.at[q, spot_b], b_s.at[ys, q], b_r.at[q, xl, zl], dev(y, xh, ys // 2, ys % 2, (xh + k) % 2))

    def b_stays(ys):
        return (ys == 2 * zl + xl) & (xh == 0)

    lag_x, lag_z, lag_a = 2, 4, 6

    def step(n, carry):
        @pl.when(n < steps)
        def _():
            t, q, dy = where_of(n)
            yp = (y + dy) % 4

            @pl.when(t == 0)
            def _():
                take_s(q)

            @pl.when(n == 1 - k)
            def _():
                cross().wait_recv()
                spread_start(lx, 1, f_s)

            @pl.when(q == 0)
            def _():
                for kk in range(2):
                    copy(lb.at[yp, kk], lb.at[yp, kk], l_s.at[0], l_r.at[yp, kk], other_core).wait_recv()
                    hi, lo = split(lb[yp, kk])
                    ahi[t, kk] = hi
                    alo[t, kk] = lo

            total = jnp.zeros((rows, width), F32)
            for kk in range(2):
                total += jnp.dot(ahi[t, kk], bhi[q, kk], preferred_element_type=F32)
                total += jnp.dot(ahi[t, kk], blo[q, kk], preferred_element_type=F32)
                total += jnp.dot(alo[t, kk], bhi[q, kk], preferred_element_type=F32)
            prod[t, q] = total
            x_copy(t, q).start()

        @pl.when((n >= lag_x) & (n < steps + lag_x))
        def _():
            t, q, _ = where_of(n - lag_x)
            x_copy(t, q).wait_recv()
            xr[t, q] = xr[t, q] + prod[t, q, pl.ds(2 * part * xl, 2 * part)]
            z_copy(t, q).start()

        @pl.when((n >= lag_z) & (n < steps + lag_z))
        def _():
            t, q, dy = where_of(n - lag_z)
            z_copy(t, q).wait_recv()
            done = -(xr[t, q, pl.ds(part * zl, part)] + zr[t, q])
            here = (t == 0) & (k == 0)

            @pl.when(here)
            def _():
                leg[y, q] = done

            @pl.when(jnp.logical_not(here))
            def _():
                fin[t, q] = done
                a_copy(t, q, dy).start()

        @pl.when(n >= lag_a)
        def _():
            t, q, dy = where_of(n - lag_a)
            ys = (y + 4 - dy) % 4

            @pl.when((t > 0) | (k > 0))
            def _():
                copy(leg.at[ys, q], leg.at[ys, q], a_s.at[0, 0], a_r.at[ys, q], other_core).wait_recv()

            @pl.when(b_stays(ys))
            def _():
                got[q, spot_b] = leg[ys, q]

            @pl.when(jnp.logical_not(b_stays(ys)))
            def _():
                b_copy(ys, q).start()
        return carry

    lax.fori_loop(0, steps + lag_a, step, 0)

    diag = [jnp.zeros((tile, tile), F32) for _ in range(rows // tile)]
    for q in range(chunks):
        for xs in range(2):
            for zs in range(2):
                here = (zs == zl) & (xs == xl) & (xh == 0)

                @pl.when(jnp.logical_not(here))
                def _():
                    spot = got.at[q, pl.ds(2 * part * xs + part * zs, part)]
                    copy(spot, spot, b_s.at[0, 0], b_r.at[q, xs, zs], other_core).wait_recv()
        cols = slice(q * width, (q + 1) * width)
        c_out[:, cols] = got[q]
        for t in range(len(diag)):
            span = slice(t * tile, (t + 1) * tile)
            diag[t] += lax.dot_general(got[q, span], l_ref[span, cols], NT, precision=lax.Precision.HIGHEST,
                                       preferred_element_type=F32)
    for t in range(len(diag)):
        dsend[:, :, t * tile:(t + 1) * tile] = diag[t].reshape(8, tile // 8, tile)

    def d_copy(d):
        to = (j + d) % 8
        return copy(dsend.at[to], dr.at[j], d_s.at[d], d_r.at[j], (me_r, half * 8 + to))

    def d_from(d):
        frm = (j + d) % 8
        return copy(dsend.at[frm], dr.at[frm], d_s.at[d], d_r.at[frm], (me_r, half * 8 + frm))

    for d in range(1, 8):
        d_copy(d).start()
    dr[j] = dsend[j]
    for d in range(1, 8):
        d_from(d).wait_recv()
    total = dr[0]
    for d in range(1, 8):
        total += dr[d]
    g[me_c] = total

    def g_copy(d):
        return copy(g.at[me_c], g.at[me_c], g_s.at[d], g_r.at[me_c], (me_r, (me_c + d) % 16))

    def g_from(d):
        frm = (me_c + d) % 16
        return copy(g.at[frm], g.at[frm], g_s.at[d], g_r.at[frm], (me_r, frm))

    for d in range(1, 16):
        g_copy(d).start()
    for d in range(1, 16):
        g_from(d).wait_recv()
    for h in range(2):
        m_out[:, h, :] = pd[:, h, :] - g[h * 8:(h + 1) * 8].reshape(tile, -1)

    cross().wait_send()
    spread_end(l_ref, 0, l_s)
    spread_end(lx, 1, f_s)
    for q in range(chunks):
        far_copy(q).wait_send()
        core_copy(k, q).wait_send()

    def sent(n, carry):
        t, q, dy = where_of(n)
        ys = (y + 4 - dy) % 4
        x_copy(t, q).wait_send()
        z_copy(t, q).wait_send()

        @pl.when((t > 0) | (k > 0))
        def _():
            a_copy(t, q, dy).wait_send()

        @pl.when(jnp.logical_not(b_stays(ys)))
        def _():
            b_copy(ys, q).wait_send()
        return carry

    lax.fori_loop(0, steps, sent, 0)
    for d in range(1, 8):
        d_copy(d).wait_send()
    for d in range(1, 16):
        g_copy(d).wait_send()


def local(root_sigma, pivot_diag, update_l, update_map):
    tile = pivot_diag.shape[0]
    rows, cols = update_l.shape
    chunks = 3
    width = cols // chunks
    sem = pltpu.SemaphoreType.DMA
    vmem = pl.BlockSpec(memory_space=pltpu.VMEM)
    return pl.pallas_call(
        kernel,
        out_shape=(jax.ShapeDtypeStruct(update_l.shape, F32), jax.ShapeDtypeStruct(pivot_diag.shape, F32)),
        in_specs=[pl.BlockSpec(memory_space=pltpu.SMEM), vmem, vmem, vmem],
        out_specs=(vmem, vmem),
        scratch_shapes=[
            pltpu.VMEM((chunks, width, cols), F32),
            pltpu.VMEM((chunks, width, cols), F32),
            pltpu.VMEM((2, chunks, cols, width), F32),
            pltpu.VMEM((chunks, 2, cols, width), BF16),
            pltpu.VMEM((chunks, 2, cols, width), BF16),
            pltpu.VMEM((rows, cols), F32),
            pltpu.VMEM((4, 2, rows, cols), F32),
            pltpu.VMEM((4, 2, rows, cols), BF16),
            pltpu.VMEM((4, 2, rows, cols), BF16),
            pltpu.VMEM((4, chunks, rows, width), F32),
            pltpu.VMEM((4, chunks, rows // 2, width), F32),
            pltpu.VMEM((4, chunks, rows // 4, width), F32),
            pltpu.VMEM((4, chunks, rows // 4, width), F32),
            pltpu.VMEM((4, chunks, rows // 4, width), F32),
            pltpu.VMEM((chunks, rows, width), F32),
            pltpu.VMEM((8, tile // 8, rows), F32),
            pltpu.VMEM((8, tile // 8, rows), F32),
            pltpu.VMEM((16, tile // 8, rows), F32),
            sem((chunks,)), sem((chunks,)), sem((chunks,)), sem((chunks,)),
            sem, sem, sem((4,)), sem((4,)), sem((4, 2)),
            sem((4, chunks)), sem((4, chunks)), sem((4, chunks)), sem((4, chunks)),
            sem((4, chunks)), sem((4, chunks)), sem((4, chunks)), sem((chunks, 2, 2)),
            sem((8,)), sem((8,)), sem((16,)), sem((16,)),
        ],
        compiler_params=pltpu.CompilerParams(
            collective_id=0, has_side_effects=True, vmem_limit_bytes=62 * 2**20),
        name="selected_inverse",
    )(update_map, root_sigma.reshape(-1, tile, root_sigma.shape[1]), pivot_diag, update_l)


def solution(mesh):
    placed = (P("prow", "pcol"), P(None, None, "prow"), P("prow", "pcol"), P())
    return jax.shard_map(
        local,
        mesh=mesh,
        in_specs=placed,
        out_specs=(P("prow", "pcol"), P(None, None, "prow")),
        check_vma=False,
    )
```

```python
import jax
import jax.numpy as jnp
from jax import lax
from jax.experimental import pallas as pl
from jax.experimental.pallas import tpu as pltpu
from jax.sharding import PartitionSpec as P

MESH = pl.DeviceIdType.MESH
F32, BF16 = jnp.float32, jnp.bfloat16
NT = (((1,), (1,)), ((), ()))


def split(x):
    hi = x.astype(BF16)
    return hi, (x - hi.astype(F32)).astype(BF16)


def kernel(umap, sig, pd, l_ref, c_out, m_out, fs, rc, stf, bhi, blo, lx, lb, ahi, alo, prod, xr, zr, fin, leg, got, dsend, dr, g,
           zs_s, zs_r, cs_s, cs_r, lx_s, lx_r, l_s, f_s, o_s, l_r, x_s, x_r, z_s, z_r, a_s, a_r, b_s, b_r, d_s, d_r, g_s, g_r):
    me_r, me_c = lax.axis_index("prow"), lax.axis_index("pcol")
    y, xh = me_r // 2, me_r % 2
    half, j = me_c // 8, me_c % 8
    zl, xl, k = j // 4, (j // 2) % 2, j % 2
    chunks, width = fs.shape[0], fs.shape[1]
    tile = sig.shape[1]
    tiles = 2 * chunks
    rows = l_ref.shape[0]
    part = rows // 4
    steps = 4 * chunks

    def dev(y_, xh_, zl_, xl_, k_):
        return (y_ * 2 + xh_, half * 8 + zl_ * 4 + xl_ * 2 + k_)

    partner = (me_r, (me_c + 8) % 16)
    other_core = dev(y, xh, zl, xl, 1 - k)
    x_peer = dev(y, xh, zl, 1 - xl, k)
    z_peer = dev(y, xh, 1 - zl, xl, k)

    def copy(src, dst, ssem, rsem, to):
        return pltpu.make_async_remote_copy(
            src_ref=src, dst_ref=dst, send_sem=ssem, recv_sem=rsem, device_id=to, device_id_type=MESH)

    barrier = pltpu.get_barrier_semaphore()

    def greet(to):
        pl.semaphore_signal(barrier, inc=1, device_id=to, device_id_type=MESH)

    for d in range(1, 16):
        greet((me_r, (me_c + d) % 16))
    for d in range(4):
        greet(dev((y + d) % 4, 1 - xh, zl, xl, k))
        if d > 0:
            for kk in range(2):
                greet(dev((y + d) % 4, xh, zl, xl, kk))
    pl.semaphore_wait(barrier, 25)

    def cross():
        return copy(l_ref, lx, lx_s, lx_r, dev(y, 1 - xh, zl, xl, k))

    def spread(src, core, sems, d):
        return copy(src, lb.at[y, k], sems.at[d], l_r.at[y, k], dev((y + d) % 4, xh, zl, xl, core))

    def spread_start(src, core, sems):
        for d in (1, 3):
            spread(src, core, sems, d).start()

        @pl.when(k != core)
        def _():
            spread(src, core, sems, 0).start()

        @pl.when(k == core)
        def _():
            pltpu.make_async_copy(src, lb.at[y, core], l_r.at[y, core]).start()

    def spread_end(src, core, sems):
        for d in (1, 3):
            spread(src, core, sems, d).wait_send()

        @pl.when(k != core)
        def _():
            spread(src, core, sems, 0).wait_send()

    def onward(t):
        yf, yt, kk = (y + 1 + 2 * (t - 1)) % 4, (y + 3 - 2 * (t - 1)) % 4, 2 - t
        return copy(lb.at[yf, kk], lb.at[yf, kk], o_s.at[t - 1], l_r.at[yf, kk], dev(yt, xh, zl, xl, k))

    cross().start()

    def far_copy(q):
        return copy(fs.at[q], rc.at[q], zs_s.at[q], zs_r.at[q], partner)

    for q in range(chunks):
        for h in range(2):
            row = umap[1 - half, me_r * tiles + 2 * q + h] // 8
            fs[q, h * tile:(h + 1) * tile, :] = sig[row]
        far_copy(q).start()

    spread_start(l_ref, 0, l_s)

    def core_copy(kk, q):
        return copy(stf.at[kk, q], stf.at[kk, q], cs_s.at[q], cs_r.at[q], other_core)

    def take_s(q):
        far_copy(q).wait_recv()
        for h in range(2):
            row = umap[half, me_r * tiles + 2 * q + h] // 8
            near = sig[row]
            far = rc[q, h * tile:(h + 1) * tile, :]
            for s in range(tiles):
                col = umap[half, j * tiles + s]
                spot = col // 16 + tiles * (((col // 8) % 2 + half) % 2)
                x = near[:, :tile]
                for c in range(1, 2 * tiles):
                    lanes = slice((c % tiles) * tile, (c % tiles + 1) * tile)
                    x = jnp.where(spot == c, (near if c < tiles else far)[:, lanes], x)
                stf[k, q, s * tile:(s + 1) * tile, h * tile:(h + 1) * tile] = x.T
        core_copy(k, q).start()
        hi, lo = split(stf[k, q])
        bhi[q, k] = hi
        blo[q, k] = lo
        core_copy(1 - k, q).wait_recv()
        hi, lo = split(stf[1 - k, q])
        bhi[q, 1 - k] = hi
        blo[q, 1 - k] = lo

    def where_of(n):
        last = n // (3 * chunks)
        t = (1 - k) * ((1 - last) * (n % 3) + last * 3) + k * (n // chunks)
        q = (1 - k) * ((1 - last) * (n // 3) + last * (n - 3 * chunks)) + k * (n % chunks)
        return t, q, t + (t // 2) * (1 - 2 * (t % 2))

    def x_copy(t, q):
        return copy(prod.at[t, q, pl.ds(2 * part * (1 - xl), 2 * part)], xr.at[t, q], x_s.at[t, q], x_r.at[t, q], x_peer)

    def z_copy(t, q):
        return copy(xr.at[t, q, pl.ds(part * (1 - zl), part)], zr.at[t, q], z_s.at[t, q], z_r.at[t, q], z_peer)

    def a_copy(t, q, dy):
        return copy(fin.at[t, q], leg.at[y, q], a_s.at[t, q], a_r.at[y, q], dev((y + dy) % 4, (xh + k) % 2, zl, xl, k))

    spot_b = pl.ds(2 * part * xl + part * zl, part)

    def b_copy(ys, q):
        return copy(leg.at[ys, q], got.at[q, spot_b], b_s.at[ys, q], b_r.at[q, xl, zl], dev(y, xh, ys // 2, ys % 2, (xh + k) % 2))

    def b_stays(ys):
        return (ys == 2 * zl + xl) & (xh == 0)

    lag_x, lag_z, lag_a = 2, 4, 6

    def step(n, carry):
        @pl.when(n < steps)
        def _():
            t, q, dy = where_of(n)
            yp = (y + dy) % 4

            @pl.when(t == 0)
            def _():
                take_s(q)

            @pl.when(n == 1 - k)
            def _():
                cross().wait_recv()
                spread_start(lx, 1, f_s)

            @pl.when(q == 0)
            def _():
                for kk in range(2):
                    copy(lb.at[yp, kk], lb.at[yp, kk], l_s.at[0], l_r.at[yp, kk], other_core).wait_recv()
                    hi, lo = split(lb[yp, kk])
                    ahi[t, kk] = hi
                    alo[t, kk] = lo

                @pl.when((t == 1) | (t == 2))
                def _():
                    onward(t).start()

            total = jnp.zeros((rows, width), F32)
            for kk in range(2):
                total += jnp.dot(ahi[t, kk], bhi[q, kk], preferred_element_type=F32)
                total += jnp.dot(ahi[t, kk], blo[q, kk], preferred_element_type=F32)
                total += jnp.dot(alo[t, kk], bhi[q, kk], preferred_element_type=F32)
            prod[t, q] = total
            x_copy(t, q).start()

        @pl.when((n >= lag_x) & (n < steps + lag_x))
        def _():
            t, q, _ = where_of(n - lag_x)
            x_copy(t, q).wait_recv()
            xr[t, q] = xr[t, q] + prod[t, q, pl.ds(2 * part * xl, 2 * part)]
            z_copy(t, q).start()

        @pl.when((n >= lag_z) & (n < steps + lag_z))
        def _():
            t, q, dy = where_of(n - lag_z)
            z_copy(t, q).wait_recv()
            done = -(xr[t, q, pl.ds(part * zl, part)] + zr[t, q])
            here = (t == 0) & (k == 0)

            @pl.when(here)
            def _():
                leg[y, q] = done

            @pl.when(jnp.logical_not(here))
            def _():
                fin[t, q] = done
                a_copy(t, q, dy).start()

        @pl.when(n >= lag_a)
        def _():
            t, q, dy = where_of(n - lag_a)
            ys = (y + 4 - dy) % 4

            @pl.when((t > 0) | (k > 0))
            def _():
                copy(leg.at[ys, q], leg.at[ys, q], a_s.at[0, 0], a_r.at[ys, q], other_core).wait_recv()

            @pl.when(b_stays(ys))
            def _():
                got[q, spot_b] = leg[ys, q]

            @pl.when(jnp.logical_not(b_stays(ys)))
            def _():
                b_copy(ys, q).start()
        return carry

    lax.fori_loop(0, steps + lag_a, step, 0)

    diag = [jnp.zeros((tile, tile), F32) for _ in range(rows // tile)]
    for q in range(chunks):
        for xs in range(2):
            for zs in range(2):
                here = (zs == zl) & (xs == xl) & (xh == 0)

                @pl.when(jnp.logical_not(here))
                def _():
                    spot = got.at[q, pl.ds(2 * part * xs + part * zs, part)]
                    copy(spot, spot, b_s.at[0, 0], b_r.at[q, xs, zs], other_core).wait_recv()
        cols = slice(q * width, (q + 1) * width)
        c_out[:, cols] = got[q]
        for t in range(len(diag)):
            span = slice(t * tile, (t + 1) * tile)
            diag[t] += lax.dot_general(got[q, span], l_ref[span, cols], NT, precision=lax.Precision.HIGHEST,
                                       preferred_element_type=F32)
    for t in range(len(diag)):
        dsend[:, :, t * tile:(t + 1) * tile] = diag[t].reshape(8, tile // 8, tile)

    def d_copy(d):
        to = (j + d) % 8
        return copy(dsend.at[to], dr.at[j], d_s.at[d], d_r.at[j], (me_r, half * 8 + to))

    def d_from(d):
        frm = (j + d) % 8
        return copy(dsend.at[frm], dr.at[frm], d_s.at[d], d_r.at[frm], (me_r, half * 8 + frm))

    for d in range(1, 8):
        d_copy(d).start()
    dr[j] = dsend[j]
    for d in range(1, 8):
        d_from(d).wait_recv()
    total = dr[0]
    for d in range(1, 8):
        total += dr[d]
    g[me_c] = total

    def g_copy(d):
        return copy(g.at[me_c], g.at[me_c], g_s.at[d], g_r.at[me_c], (me_r, (me_c + d) % 16))

    def g_from(d):
        frm = (me_c + d) % 16
        return copy(g.at[frm], g.at[frm], g_s.at[d], g_r.at[frm], (me_r, frm))

    for d in range(1, 16):
        g_copy(d).start()
    for d in range(1, 16):
        g_from(d).wait_recv()
    for h in range(2):
        m_out[:, h, :] = pd[:, h, :] - g[h * 8:(h + 1) * 8].reshape(tile, -1)

    cross().wait_send()
    spread_end(l_ref, 0, l_s)
    spread_end(lx, 1, f_s)
    for t in (1, 2):
        onward(t).wait_send()
    for q in range(chunks):
        far_copy(q).wait_send()
        core_copy(k, q).wait_send()

    def sent(n, carry):
        t, q, dy = where_of(n)
        ys = (y + 4 - dy) % 4
        x_copy(t, q).wait_send()
        z_copy(t, q).wait_send()

        @pl.when((t > 0) | (k > 0))
        def _():
            a_copy(t, q, dy).wait_send()

        @pl.when(jnp.logical_not(b_stays(ys)))
        def _():
            b_copy(ys, q).wait_send()
        return carry

    lax.fori_loop(0, steps, sent, 0)
    for d in range(1, 8):
        d_copy(d).wait_send()
    for d in range(1, 16):
        g_copy(d).wait_send()


def local(root_sigma, pivot_diag, update_l, update_map):
    tile = pivot_diag.shape[0]
    rows, cols = update_l.shape
    chunks = 3
    width = cols // chunks
    sem = pltpu.SemaphoreType.DMA
    vmem = pl.BlockSpec(memory_space=pltpu.VMEM)
    return pl.pallas_call(
        kernel,
        out_shape=(jax.ShapeDtypeStruct(update_l.shape, F32), jax.ShapeDtypeStruct(pivot_diag.shape, F32)),
        in_specs=[pl.BlockSpec(memory_space=pltpu.SMEM), vmem, vmem, vmem],
        out_specs=(vmem, vmem),
        scratch_shapes=[
            pltpu.VMEM((chunks, width, cols), F32),
            pltpu.VMEM((chunks, width, cols), F32),
            pltpu.VMEM((2, chunks, cols, width), F32),
            pltpu.VMEM((chunks, 2, cols, width), BF16),
            pltpu.VMEM((chunks, 2, cols, width), BF16),
            pltpu.VMEM((rows, cols), F32),
            pltpu.VMEM((4, 2, rows, cols), F32),
            pltpu.VMEM((4, 2, rows, cols), BF16),
            pltpu.VMEM((4, 2, rows, cols), BF16),
            pltpu.VMEM((4, chunks, rows, width), F32),
            pltpu.VMEM((4, chunks, rows // 2, width), F32),
            pltpu.VMEM((4, chunks, rows // 4, width), F32),
            pltpu.VMEM((4, chunks, rows // 4, width), F32),
            pltpu.VMEM((4, chunks, rows // 4, width), F32),
            pltpu.VMEM((chunks, rows, width), F32),
            pltpu.VMEM((8, tile // 8, rows), F32),
            pltpu.VMEM((8, tile // 8, rows), F32),
            pltpu.VMEM((16, tile // 8, rows), F32),
            sem((chunks,)), sem((chunks,)), sem((chunks,)), sem((chunks,)),
            sem, sem, sem((4,)), sem((4,)), sem((2,)), sem((4, 2)),
            sem((4, chunks)), sem((4, chunks)), sem((4, chunks)), sem((4, chunks)),
            sem((4, chunks)), sem((4, chunks)), sem((4, chunks)), sem((chunks, 2, 2)),
            sem((8,)), sem((8,)), sem((16,)), sem((16,)),
        ],
        compiler_params=pltpu.CompilerParams(
            collective_id=0, has_side_effects=True, vmem_limit_bytes=62 * 2**20),
        name="selected_inverse",
    )(update_map, root_sigma.reshape(-1, tile, root_sigma.shape[1]), pivot_diag, update_l)


def solution(mesh):
    placed = (P("prow", "pcol"), P(None, None, "prow"), P("prow", "pcol"), P())
    return jax.shard_map(
        local,
        mesh=mesh,
        in_specs=placed,
        out_specs=(P("prow", "pcol"), P(None, None, "prow")),
        check_vma=False,
    )
```

```python
import jax
import jax.numpy as jnp
from jax import lax
from jax.experimental import pallas as pl
from jax.experimental.pallas import tpu as pltpu
from jax.sharding import PartitionSpec as P

MESH = pl.DeviceIdType.MESH
F32, BF16 = jnp.float32, jnp.bfloat16
NT = (((1,), (1,)), ((), ()))


def split(x):
    hi = x.astype(BF16)
    return hi, (x - hi.astype(F32)).astype(BF16)


def kernel(umap, sig_in, pd, l_in, c_out, m_out, sig, l_ref, lhi, llo, fs, rc, stf, bhi, blo, lx, lb, ahi, alo, prod, xr, zr, fin, leg, got, dsend, dr, g,
           in_s, zs_s, zs_r, cs_s, cs_r, lx_s, lx_r, l_s, f_s, o_s, l_r, x_s, x_r, z_s, z_r, a_s, a_r, b_s, b_r, d_s, d_r, g_s, g_r):
    me_r, me_c = lax.axis_index("prow"), lax.axis_index("pcol")
    y, xh = me_r // 2, me_r % 2
    half, j = me_c // 8, me_c % 8
    zl, xl, k = j // 4, (j // 2) % 2, j % 2
    chunks, width = fs.shape[0], fs.shape[1]
    tile = sig.shape[1]
    tiles = 2 * chunks
    rows = l_ref.shape[0]
    part = rows // 4
    steps = 4 * chunks

    def dev(y_, xh_, zl_, xl_, k_):
        return (y_ * 2 + xh_, half * 8 + zl_ * 4 + xl_ * 2 + k_)

    partner = (me_r, (me_c + 8) % 16)
    other_core = dev(y, xh, zl, xl, 1 - k)

    def copy(src, dst, ssem, rsem, to):
        return pltpu.make_async_remote_copy(
            src_ref=src, dst_ref=dst, send_sem=ssem, recv_sem=rsem, device_id=to, device_id_type=MESH)

    load_l = pltpu.make_async_copy(l_in, l_ref, in_s.at[0])
    load_sig = pltpu.make_async_copy(sig_in, sig, in_s.at[1])
    load_l.start()
    load_sig.start()

    barrier = pltpu.get_barrier_semaphore()

    def greet(to):
        pl.semaphore_signal(barrier, inc=1, device_id=to, device_id_type=MESH)

    for d in range(1, 16):
        greet((me_r, (me_c + d) % 16))
    for d in range(4):
        greet(dev((y + d) % 4, 1 - xh, zl, xl, k))
        if d > 0:
            for kk in range(2):
                greet(dev((y + d) % 4, xh, zl, xl, kk))
    pl.semaphore_wait(barrier, 25)

    def cross():
        return copy(l_ref, lx, lx_s, lx_r, dev(y, 1 - xh, zl, xl, k))

    def spread(src, core, sems, d):
        return copy(src, lb.at[y, k], sems.at[d], l_r.at[y, k], dev((y + d) % 4, xh, zl, xl, core))

    def spread_start(src, core, sems):
        for d in (1, 3):
            spread(src, core, sems, d).start()

        @pl.when(k != core)
        def _():
            spread(src, core, sems, 0).start()

        @pl.when(k == core)
        def _():
            pltpu.make_async_copy(src, lb.at[y, core], l_r.at[y, core]).start()

    def spread_end(src, core, sems):
        for d in (1, 3):
            spread(src, core, sems, d).wait_send()

        @pl.when(k != core)
        def _():
            spread(src, core, sems, 0).wait_send()

    def onward(t):
        yf, yt, kk = (y + 1 + 2 * (t - 1)) % 4, (y + 3 - 2 * (t - 1)) % 4, 2 - t
        return copy(lb.at[yf, kk], lb.at[yf, kk], o_s.at[t - 1], l_r.at[yf, kk], dev(yt, xh, zl, xl, k))

    load_l.wait()
    cross().start()
    spread_start(l_ref, 0, l_s)

    def far_copy(q):
        return copy(fs.at[q], rc.at[q], zs_s.at[q], zs_r.at[q], partner)

    load_sig.wait()
    for q in range(chunks):
        for h in range(2):
            row = umap[1 - half, me_r * tiles + 2 * q + h] // 8
            fs[q, h * tile:(h + 1) * tile, :] = sig[row]
        far_copy(q).start()
    hi, lo = split(l_ref[...])
    lhi[...] = hi
    llo[...] = lo

    def core_copy(kk, q):
        return copy(stf.at[kk, q], stf.at[kk, q], cs_s.at[q], cs_r.at[q], other_core)

    def take_s(q):
        far_copy(q).wait_recv()
        for h in range(2):
            row = umap[half, me_r * tiles + 2 * q + h] // 8
            near = sig[row]
            far = rc[q, h * tile:(h + 1) * tile, :]
            for s in range(tiles):
                col = umap[half, j * tiles + s]
                spot = col // 16 + tiles * (((col // 8) % 2 + half) % 2)
                x = near[:, :tile]
                for c in range(1, 2 * tiles):
                    lanes = slice((c % tiles) * tile, (c % tiles + 1) * tile)
                    x = jnp.where(spot == c, (near if c < tiles else far)[:, lanes], x)
                stf[k, q, s * tile:(s + 1) * tile, h * tile:(h + 1) * tile] = x.T
        core_copy(k, q).start()
        hi, lo = split(stf[k, q])
        bhi[q, k] = hi
        blo[q, k] = lo
        core_copy(1 - k, q).wait_recv()
        hi, lo = split(stf[1 - k, q])
        bhi[q, 1 - k] = hi
        blo[q, 1 - k] = lo

    def where_of(n):
        last = n // (3 * chunks)
        t = (1 - k) * ((1 - last) * (n % 3) + last * 3) + k * (n // chunks)
        q = (1 - k) * ((1 - last) * (n // 3) + last * (n - 3 * chunks)) + k * (n % chunks)
        return t, q, t + (t // 2) * (1 - 2 * (t % 2))

    def order(q):
        f = q // (chunks - 1)
        return f, f * zl + (1 - f) * xl, f * xl + (1 - f) * zl

    def peer(f):
        return dev(y, xh, zl + f * (1 - 2 * zl), xl + (1 - f) * (1 - 2 * xl), k)

    def x_copy(t, q):
        f, b1, _ = order(q)
        return copy(prod.at[t, q, pl.ds(2 * part * (1 - b1), 2 * part)], xr.at[t, q], x_s.at[t, q], x_r.at[t, q], peer(f))

    def z_copy(t, q):
        f, _, b2 = order(q)
        return copy(xr.at[t, q, pl.ds(part * (1 - b2), part)], zr.at[t, q], z_s.at[t, q], z_r.at[t, q], peer(1 - f))

    def spot_of(q):
        _, b1, b2 = order(q)
        return pl.ds(2 * part * b1 + part * b2, part)

    def a_copy(t, q, dy):
        return copy(fin.at[t, q], leg.at[y, q], a_s.at[t, q], a_r.at[y, q], dev((y + dy) % 4, (xh + k) % 2, zl, xl, k))

    def b_copy(ys, q):
        _, b1, b2 = order(q)
        return copy(leg.at[ys, q], got.at[q, spot_of(q)], b_s.at[ys, q], b_r.at[q, b1, b2], dev(y, xh, ys // 2, ys % 2, (xh + k) % 2))

    def b_stays(ys):
        return (ys == 2 * zl + xl) & (xh == 0)

    lag_x, lag_z, lag_a = 2, 4, 6
    gap_1, gap_2 = 2, 4
    turns = steps + gap_1 + gap_2

    def at_turn(v):
        after_1 = jnp.where(v >= chunks + gap_1, 1, 0)
        after_2 = jnp.where(v >= 3 * chunks + gap_1 + gap_2, 1, 0)
        n = v - gap_1 * after_1 - gap_2 * after_2
        busy = (v >= 0) & (n < chunks + (2 * chunks) * after_1 + chunks * after_2)
        return busy, n

    def turn(v, carry):
        busy, n = at_turn(v - lag_a)

        @pl.when(busy)
        def _():
            t, q, dy = where_of(n)
            ys = (y + 4 - dy) % 4

            @pl.when((t > 0) | (k > 0))
            def _():
                copy(leg.at[ys, q], leg.at[ys, q], a_s.at[0, 0], a_r.at[ys, q], other_core).wait_recv()

            @pl.when(b_stays(ys))
            def _():
                got[q, spot_of(q)] = leg[ys, q]

            @pl.when(jnp.logical_not(b_stays(ys)))
            def _():
                b_copy(ys, q).start()

        busy, n = at_turn(v - lag_z)

        @pl.when(busy)
        def _():
            t, q, dy = where_of(n)
            _, _, b2 = order(q)
            z_copy(t, q).wait_recv()
            done = -(xr[t, q, pl.ds(part * b2, part)] + zr[t, q])
            here = (t == 0) & (k == 0)

            @pl.when(here)
            def _():
                leg[y, q] = done

            @pl.when(jnp.logical_not(here))
            def _():
                fin[t, q] = done
                a_copy(t, q, dy).start()

        busy, n = at_turn(v - lag_x)

        @pl.when(busy)
        def _():
            t, q, _ = where_of(n)
            _, b1, _ = order(q)
            x_copy(t, q).wait_recv()
            xr[t, q] = xr[t, q] + prod[t, q, pl.ds(2 * part * b1, 2 * part)]
            z_copy(t, q).start()

        busy, n = at_turn(v)

        @pl.when(busy)
        def _():
            t, q, dy = where_of(n)
            yp = (y + dy) % 4

            @pl.when(t == 0)
            def _():
                take_s(q)

            @pl.when(n == 1 - k)
            def _():
                cross().wait_recv()
                spread_start(lx, 1, f_s)

            @pl.when(q == 0)
            def _():
                for kk in range(2):
                    copy(lb.at[yp, kk], lb.at[yp, kk], l_s.at[0], l_r.at[yp, kk], other_core).wait_recv()

                @pl.when((t == 1) | (t == 2))
                def _():
                    onward(t).start()

                for kk in range(2):
                    hi, lo = split(lb[yp, kk])
                    ahi[t, kk] = hi
                    alo[t, kk] = lo

            total = jnp.zeros((rows, width), F32)
            for kk in range(2):
                total += jnp.dot(ahi[t, kk], bhi[q, kk], preferred_element_type=F32)
                total += jnp.dot(ahi[t, kk], blo[q, kk], preferred_element_type=F32)
                total += jnp.dot(alo[t, kk], bhi[q, kk], preferred_element_type=F32)
            prod[t, q] = total
            x_copy(t, q).start()
        return carry

    lax.fori_loop(0, turns + lag_a, turn, 0)

    diag = [jnp.zeros((tile, tile), F32) for _ in range(rows // tile)]
    for q in range(chunks):
        _, b1, b2 = order(q)
        for u in range(2):
            for v in range(2):
                @pl.when(jnp.logical_not((u == b1) & (v == b2) & (xh == 0)))
                def _():
                    spot = got.at[q, pl.ds(2 * part * u + part * v, part)]
                    copy(spot, spot, b_s.at[0, 0], b_r.at[q, u, v], other_core).wait_recv()
        cols = slice(q * width, (q + 1) * width)
        c_out[:, cols] = got[q]
        for t in range(len(diag)):
            span = slice(t * tile, (t + 1) * tile)
            hi, lo = split(got[q, span])
            for left, right in ((hi, lhi), (hi, llo), (lo, lhi)):
                diag[t] += lax.dot_general(left, right[span, cols], NT, preferred_element_type=F32)
    for t in range(len(diag)):
        dsend[:, :, t * tile:(t + 1) * tile] = diag[t].reshape(8, tile // 8, tile)

    def d_copy(d):
        to = (j + d) % 8
        return copy(dsend.at[to], dr.at[j], d_s.at[d], d_r.at[j], (me_r, half * 8 + to))

    def d_from(d):
        frm = (j + d) % 8
        return copy(dsend.at[frm], dr.at[frm], d_s.at[d], d_r.at[frm], (me_r, half * 8 + frm))

    for d in range(1, 8):
        d_copy(d).start()
    dr[j] = dsend[j]
    for d in range(1, 8):
        d_from(d).wait_recv()
    total = dr[0]
    for d in range(1, 8):
        total += dr[d]
    g[me_c] = total

    def g_copy(d):
        return copy(g.at[me_c], g.at[me_c], g_s.at[d], g_r.at[me_c], (me_r, (me_c + d) % 16))

    def g_from(d):
        frm = (me_c + d) % 16
        return copy(g.at[frm], g.at[frm], g_s.at[d], g_r.at[frm], (me_r, frm))

    for d in range(1, 16):
        g_copy(d).start()
    for d in range(1, 16):
        g_from(d).wait_recv()
    for h in range(2):
        m_out[:, h, :] = pd[:, h, :] - g[h * 8:(h + 1) * 8].reshape(tile, -1)

    cross().wait_send()
    spread_end(l_ref, 0, l_s)
    spread_end(lx, 1, f_s)
    for t in (1, 2):
        onward(t).wait_send()
    for q in range(chunks):
        far_copy(q).wait_send()
        core_copy(k, q).wait_send()

    def sent(n, carry):
        t, q, dy = where_of(n)
        ys = (y + 4 - dy) % 4
        x_copy(t, q).wait_send()
        z_copy(t, q).wait_send()

        @pl.when((t > 0) | (k > 0))
        def _():
            a_copy(t, q, dy).wait_send()

        @pl.when(jnp.logical_not(b_stays(ys)))
        def _():
            b_copy(ys, q).wait_send()
        return carry

    lax.fori_loop(0, steps, sent, 0)
    for d in range(1, 8):
        d_copy(d).wait_send()
    for d in range(1, 16):
        g_copy(d).wait_send()


def local(root_sigma, pivot_diag, update_l, update_map):
    tile = pivot_diag.shape[0]
    rows, cols = update_l.shape
    chunks = 3
    width = cols // chunks
    sem = pltpu.SemaphoreType.DMA
    vmem = pl.BlockSpec(memory_space=pltpu.VMEM)
    anywhere = pl.BlockSpec(memory_space=pl.ANY)
    return pl.pallas_call(
        kernel,
        out_shape=(jax.ShapeDtypeStruct(update_l.shape, F32), jax.ShapeDtypeStruct(pivot_diag.shape, F32)),
        in_specs=[pl.BlockSpec(memory_space=pltpu.SMEM), anywhere, vmem, anywhere],
        out_specs=(vmem, vmem),
        scratch_shapes=[
            pltpu.VMEM((root_sigma.shape[0] // tile, tile, root_sigma.shape[1]), F32),
            pltpu.VMEM((rows, cols), F32),
            pltpu.VMEM((rows, cols), BF16),
            pltpu.VMEM((rows, cols), BF16),
            pltpu.VMEM((chunks, width, cols), F32),
            pltpu.VMEM((chunks, width, cols), F32),
            pltpu.VMEM((2, chunks, cols, width), F32),
            pltpu.VMEM((chunks, 2, cols, width), BF16),
            pltpu.VMEM((chunks, 2, cols, width), BF16),
            pltpu.VMEM((rows, cols), F32),
            pltpu.VMEM((4, 2, rows, cols), F32),
            pltpu.VMEM((4, 2, rows, cols), BF16),
            pltpu.VMEM((4, 2, rows, cols), BF16),
            pltpu.VMEM((4, chunks, rows, width), F32),
            pltpu.VMEM((4, chunks, rows // 2, width), F32),
            pltpu.VMEM((4, chunks, rows // 4, width), F32),
            pltpu.VMEM((4, chunks, rows // 4, width), F32),
            pltpu.VMEM((4, chunks, rows // 4, width), F32),
            pltpu.VMEM((chunks, rows, width), F32),
            pltpu.VMEM((8, tile // 8, rows), F32),
            pltpu.VMEM((8, tile // 8, rows), F32),
            pltpu.VMEM((16, tile // 8, rows), F32),
            sem((2,)),
            sem((chunks,)), sem((chunks,)), sem((chunks,)), sem((chunks,)),
            sem, sem, sem((4,)), sem((4,)), sem((2,)), sem((4, 2)),
            sem((4, chunks)), sem((4, chunks)), sem((4, chunks)), sem((4, chunks)),
            sem((4, chunks)), sem((4, chunks)), sem((4, chunks)), sem((chunks, 2, 2)),
            sem((8,)), sem((8,)), sem((16,)), sem((16,)),
        ],
        compiler_params=pltpu.CompilerParams(
            collective_id=0, has_side_effects=True, vmem_limit_bytes=62 * 2**20),
        name="selected_inverse",
    )(update_map, root_sigma.reshape(-1, tile, root_sigma.shape[1]), pivot_diag, update_l)


def solution(mesh):
    placed = (P("prow", "pcol"), P(None, None, "prow"), P("prow", "pcol"), P())
    return jax.shard_map(
        local,
        mesh=mesh,
        in_specs=placed,
        out_specs=(P("prow", "pcol"), P(None, None, "prow")),
        check_vma=False,
    )
```

```python
import jax
import jax.numpy as jnp
from jax import lax
from jax.experimental import pallas as pl
from jax.experimental.pallas import tpu as pltpu
from jax.sharding import PartitionSpec as P

MESH = pl.DeviceIdType.MESH
F32, BF16 = jnp.float32, jnp.bfloat16
NT = (((1,), (1,)), ((), ()))


def split(x):
    hi = x.astype(BF16)
    return hi, (x - hi.astype(F32)).astype(BF16)


def kernel(umap, sig_in, pd, l_in, c_out, m_out, sig, l_ref, lhi, llo, fs, rc, stf, bhi, blo, lx, lb, ahi, alo, prod, xr, zr, fin, leg, got, dsend, dr, g,
           in_s, zs_s, zs_r, cs_s, cs_r, lx_s, lx_r, l_s, f_s, o_s, l_r, x_s, x_r, z_s, z_r, a_s, a_r, b_s, b_r, d_s, d_r, g_s, g_r):
    me_r, me_c = lax.axis_index("prow"), lax.axis_index("pcol")
    y, xh = me_r // 2, me_r % 2
    half, j = me_c // 8, me_c % 8
    zl, xl, k = j // 4, (j // 2) % 2, j % 2
    chunks, width = fs.shape[0], fs.shape[1]
    tile = sig.shape[1]
    tiles = 2 * chunks
    rows = l_ref.shape[0]
    part = rows // 4
    steps = 4 * chunks

    def dev(y_, xh_, zl_, xl_, k_):
        return (y_ * 2 + xh_, half * 8 + zl_ * 4 + xl_ * 2 + k_)

    partner = (me_r, (me_c + 8) % 16)
    other_core = dev(y, xh, zl, xl, 1 - k)

    def copy(src, dst, ssem, rsem, to):
        return pltpu.make_async_remote_copy(
            src_ref=src, dst_ref=dst, send_sem=ssem, recv_sem=rsem, device_id=to, device_id_type=MESH)

    load_l = pltpu.make_async_copy(l_in, l_ref, in_s.at[0])
    load_sig = pltpu.make_async_copy(sig_in, sig, in_s.at[1])
    load_l.start()
    load_sig.start()

    barrier = pltpu.get_barrier_semaphore()

    def greet(to):
        pl.semaphore_signal(barrier, inc=1, device_id=to, device_id_type=MESH)

    for d in range(1, 16):
        greet((me_r, (me_c + d) % 16))
    for d in range(1, 4):
        for kk in range(2):
            greet(dev((y + d) % 4, xh, zl, xl, kk))
    for d in range(8):
        greet((2 * y + 1 - xh, half * 8 + d))
    pl.semaphore_wait(barrier, 29)

    def cross():
        return copy(l_ref, lx, lx_s, lx_r, dev(y, 1 - xh, zl, xl, k))

    def spread(src, core, sems, d):
        return copy(src, lb.at[y, k], sems.at[d], l_r.at[y, k], dev((y + d) % 4, xh, zl, xl, core))

    def spread_start(src, core, sems):
        for d in (1, 3):
            spread(src, core, sems, d).start()

        @pl.when(k != core)
        def _():
            spread(src, core, sems, 0).start()

        @pl.when(k == core)
        def _():
            pltpu.make_async_copy(src, lb.at[y, core], l_r.at[y, core]).start()

    def spread_end(src, core, sems):
        for d in (1, 3):
            spread(src, core, sems, d).wait_send()

        @pl.when(k != core)
        def _():
            spread(src, core, sems, 0).wait_send()

    def onward(t):
        yf, yt, kk = (y + 1 + 2 * (t - 1)) % 4, (y + 3 - 2 * (t - 1)) % 4, 2 - t
        return copy(lb.at[yf, kk], lb.at[yf, kk], o_s.at[t - 1], l_r.at[yf, kk], dev(yt, xh, zl, xl, k))

    load_l.wait()
    cross().start()
    spread_start(l_ref, 0, l_s)

    def far_copy(q):
        return copy(fs.at[q], rc.at[q], zs_s.at[q], zs_r.at[q], partner)

    load_sig.wait()
    for q in range(chunks):
        for h in range(2):
            row = umap[1 - half, me_r * tiles + 2 * q + h] // 8
            fs[q, h * tile:(h + 1) * tile, :] = sig[row]
        far_copy(q).start()
    hi, lo = split(l_ref[...])
    lhi[...] = hi
    llo[...] = lo

    def core_copy(kk, q):
        return copy(stf.at[kk, q], stf.at[kk, q], cs_s.at[q], cs_r.at[q], other_core)

    def take_s(q):
        far_copy(q).wait_recv()
        for h in range(2):
            row = umap[half, me_r * tiles + 2 * q + h] // 8
            near = sig[row]
            far = rc[q, h * tile:(h + 1) * tile, :]
            for s in range(tiles):
                col = umap[half, j * tiles + s]
                spot = col // 16 + tiles * (((col // 8) % 2 + half) % 2)
                x = near[:, :tile]
                for c in range(1, 2 * tiles):
                    lanes = slice((c % tiles) * tile, (c % tiles + 1) * tile)
                    x = jnp.where(spot == c, (near if c < tiles else far)[:, lanes], x)
                stf[k, q, s * tile:(s + 1) * tile, h * tile:(h + 1) * tile] = x.T
        core_copy(k, q).start()
        hi, lo = split(stf[k, q])
        bhi[q, k] = hi
        blo[q, k] = lo
        core_copy(1 - k, q).wait_recv()
        hi, lo = split(stf[1 - k, q])
        bhi[q, 1 - k] = hi
        blo[q, 1 - k] = lo

    def where_of(n):
        last = n // (3 * chunks)
        t = (1 - k) * ((1 - last) * (n % 3) + last * 3) + k * (n // chunks)
        q = (1 - k) * ((1 - last) * (n // 3) + last * (n - 3 * chunks)) + k * (n % chunks)
        return t, q, t + (t // 2) * (1 - 2 * (t % 2))

    def order(q):
        f = q // (chunks - 1)
        return f, f * zl + (1 - f) * xl, f * xl + (1 - f) * zl

    def peer(f):
        return dev(y, xh, zl + f * (1 - 2 * zl), xl + (1 - f) * (1 - 2 * xl), k)

    def x_copy(t, q):
        f, b1, _ = order(q)
        return copy(prod.at[t, q, pl.ds(2 * part * (1 - b1), 2 * part)], xr.at[t, q], x_s.at[t, q], x_r.at[t, q], peer(f))

    def z_copy(t, q):
        f, _, b2 = order(q)
        return copy(xr.at[t, q, pl.ds(part * (1 - b2), part)], zr.at[t, q], z_s.at[t, q], z_r.at[t, q], peer(1 - f))

    def spot_of(q):
        _, b1, b2 = order(q)
        return pl.ds(2 * part * b1 + part * b2, part)

    def a_copy(t, q, dy):
        return copy(fin.at[t, q], leg.at[y, q], a_s.at[t, q], a_r.at[y, q], dev((y + dy) % 4, xh, zl, xl, k))

    def b_copy(ys, q):
        _, b1, b2 = order(q)
        to = dev(y, (xh + k) % 2, ys // 2, ys % 2, xh)
        return copy(leg.at[ys, q], got.at[q, spot_of(q)], b_s.at[ys, q], b_r.at[q, b1, b2], to)

    def b_stays(ys):
        return (ys == 2 * zl + xl) & (xh == 0) & (k == 0)

    lag_x, lag_z, lag_a = 2, 4, 8

    def at_turn(v):
        return (v >= 0) & (v < steps), v

    def turn(v, carry):
        busy, n = at_turn(v)

        @pl.when(busy)
        def _():
            t, q, dy = where_of(n)
            yp = (y + dy) % 4

            @pl.when(t == 0)
            def _():
                take_s(q)

            @pl.when(n == 1 - k)
            def _():
                cross().wait_recv()
                spread_start(lx, 1, f_s)

            @pl.when(q == 0)
            def _():
                for kk in range(2):
                    copy(lb.at[yp, kk], lb.at[yp, kk], l_s.at[0], l_r.at[yp, kk], other_core).wait_recv()

                @pl.when((t == 1) | (t == 2))
                def _():
                    onward(t).start()

                for kk in range(2):
                    hi, lo = split(lb[yp, kk])
                    ahi[t, kk] = hi
                    alo[t, kk] = lo

            total = jnp.zeros((rows, width), F32)
            for kk in range(2):
                total += jnp.dot(ahi[t, kk], bhi[q, kk], preferred_element_type=F32)
                total += jnp.dot(ahi[t, kk], blo[q, kk], preferred_element_type=F32)
                total += jnp.dot(alo[t, kk], bhi[q, kk], preferred_element_type=F32)
            prod[t, q] = total
            x_copy(t, q).start()

        busy, n = at_turn(v - lag_x)

        @pl.when(busy)
        def _():
            t, q, _ = where_of(n)
            _, b1, _ = order(q)
            x_copy(t, q).wait_recv()
            xr[t, q] = xr[t, q] + prod[t, q, pl.ds(2 * part * b1, 2 * part)]
            z_copy(t, q).start()

        busy, n = at_turn(v - lag_z)

        @pl.when(busy)
        def _():
            t, q, dy = where_of(n)
            _, _, b2 = order(q)
            z_copy(t, q).wait_recv()
            done = -(xr[t, q, pl.ds(part * b2, part)] + zr[t, q])

            @pl.when(t == 0)
            def _():
                leg[y, q] = done

            @pl.when(t > 0)
            def _():
                fin[t, q] = done
                a_copy(t, q, dy).start()

        busy, n = at_turn(v - lag_a)

        @pl.when(busy)
        def _():
            t, q, dy = where_of(n)
            ys = (y + 4 - dy) % 4

            @pl.when(t > 0)
            def _():
                copy(leg.at[ys, q], leg.at[ys, q], a_s.at[0, 0], a_r.at[ys, q], other_core).wait_recv()

            @pl.when(b_stays(ys))
            def _():
                got[q, spot_of(q)] = leg[ys, q]

            @pl.when(jnp.logical_not(b_stays(ys)))
            def _():
                b_copy(ys, q).start()
        return carry

    lax.fori_loop(0, steps + lag_a, turn, 0)

    diag = [jnp.zeros((tile, tile), F32) for _ in range(rows // tile)]
    for q in range(chunks):
        _, b1, b2 = order(q)
        for u in range(2):
            for v in range(2):
                @pl.when(jnp.logical_not((u == b1) & (v == b2) & (xh == 0) & (k == 0)))
                def _():
                    spot = got.at[q, pl.ds(2 * part * u + part * v, part)]
                    copy(spot, spot, b_s.at[0, 0], b_r.at[q, u, v], other_core).wait_recv()
        cols = slice(q * width, (q + 1) * width)
        c_out[:, cols] = got[q]
        for t in range(len(diag)):
            span = slice(t * tile, (t + 1) * tile)
            hi, lo = split(got[q, span])
            for left, right in ((hi, lhi), (hi, llo), (lo, lhi)):
                diag[t] += lax.dot_general(left, right[span, cols], NT, preferred_element_type=F32)
    for t in range(len(diag)):
        dsend[:, :, t * tile:(t + 1) * tile] = diag[t].reshape(8, tile // 8, tile)

    def d_copy(d):
        to = (j + d) % 8
        return copy(dsend.at[to], dr.at[j], d_s.at[d], d_r.at[j], (me_r, half * 8 + to))

    def d_from(d):
        frm = (j + d) % 8
        return copy(dsend.at[frm], dr.at[frm], d_s.at[d], d_r.at[frm], (me_r, half * 8 + frm))

    for d in range(1, 8):
        d_copy(d).start()
    dr[j] = dsend[j]
    for d in range(1, 8):
        d_from(d).wait_recv()
    total = dr[0]
    for d in range(1, 8):
        total += dr[d]
    g[me_c] = total

    def g_copy(d):
        return copy(g.at[me_c], g.at[me_c], g_s.at[d], g_r.at[me_c], (me_r, (me_c + d) % 16))

    def g_from(d):
        frm = (me_c + d) % 16
        return copy(g.at[frm], g.at[frm], g_s.at[d], g_r.at[frm], (me_r, frm))

    for d in range(1, 16):
        g_copy(d).start()
    for d in range(1, 16):
        g_from(d).wait_recv()
    for h in range(2):
        m_out[:, h, :] = pd[:, h, :] - g[h * 8:(h + 1) * 8].reshape(tile, -1)

    cross().wait_send()
    spread_end(l_ref, 0, l_s)
    spread_end(lx, 1, f_s)
    for t in (1, 2):
        onward(t).wait_send()
    for q in range(chunks):
        far_copy(q).wait_send()
        core_copy(k, q).wait_send()

    def sent(n, carry):
        t, q, dy = where_of(n)
        ys = (y + 4 - dy) % 4
        x_copy(t, q).wait_send()
        z_copy(t, q).wait_send()

        @pl.when(t > 0)
        def _():
            a_copy(t, q, dy).wait_send()

        @pl.when(jnp.logical_not(b_stays(ys)))
        def _():
            b_copy(ys, q).wait_send()
        return carry

    lax.fori_loop(0, steps, sent, 0)
    for d in range(1, 8):
        d_copy(d).wait_send()
    for d in range(1, 16):
        g_copy(d).wait_send()


def local(root_sigma, pivot_diag, update_l, update_map):
    tile = pivot_diag.shape[0]
    rows, cols = update_l.shape
    chunks = 3
    width = cols // chunks
    sem = pltpu.SemaphoreType.DMA
    vmem = pl.BlockSpec(memory_space=pltpu.VMEM)
    anywhere = pl.BlockSpec(memory_space=pl.ANY)
    return pl.pallas_call(
        kernel,
        out_shape=(jax.ShapeDtypeStruct(update_l.shape, F32), jax.ShapeDtypeStruct(pivot_diag.shape, F32)),
        in_specs=[pl.BlockSpec(memory_space=pltpu.SMEM), anywhere, vmem, anywhere],
        out_specs=(vmem, vmem),
        scratch_shapes=[
            pltpu.VMEM((root_sigma.shape[0] // tile, tile, root_sigma.shape[1]), F32),
            pltpu.VMEM((rows, cols), F32),
            pltpu.VMEM((rows, cols), BF16),
            pltpu.VMEM((rows, cols), BF16),
            pltpu.VMEM((chunks, width, cols), F32),
            pltpu.VMEM((chunks, width, cols), F32),
            pltpu.VMEM((2, chunks, cols, width), F32),
            pltpu.VMEM((chunks, 2, cols, width), BF16),
            pltpu.VMEM((chunks, 2, cols, width), BF16),
            pltpu.VMEM((rows, cols), F32),
            pltpu.VMEM((4, 2, rows, cols), F32),
            pltpu.VMEM((4, 2, rows, cols), BF16),
            pltpu.VMEM((4, 2, rows, cols), BF16),
            pltpu.VMEM((4, chunks, rows, width), F32),
            pltpu.VMEM((4, chunks, rows // 2, width), F32),
            pltpu.VMEM((4, chunks, rows // 4, width), F32),
            pltpu.VMEM((4, chunks, rows // 4, width), F32),
            pltpu.VMEM((4, chunks, rows // 4, width), F32),
            pltpu.VMEM((chunks, rows, width), F32),
            pltpu.VMEM((8, tile // 8, rows), F32),
            pltpu.VMEM((8, tile // 8, rows), F32),
            pltpu.VMEM((16, tile // 8, rows), F32),
            sem((2,)),
            sem((chunks,)), sem((chunks,)), sem((chunks,)), sem((chunks,)),
            sem, sem, sem((4,)), sem((4,)), sem((2,)), sem((4, 2)),
            sem((4, chunks)), sem((4, chunks)), sem((4, chunks)), sem((4, chunks)),
            sem((4, chunks)), sem((4, chunks)), sem((4, chunks)), sem((chunks, 2, 2)),
            sem((8,)), sem((8,)), sem((16,)), sem((16,)),
        ],
        compiler_params=pltpu.CompilerParams(
            collective_id=0, has_side_effects=True, vmem_limit_bytes=62 * 2**20),
        name="selected_inverse",
    )(update_map, root_sigma.reshape(-1, tile, root_sigma.shape[1]), pivot_diag, update_l)


def solution(mesh):
    placed = (P("prow", "pcol"), P(None, None, "prow"), P("prow", "pcol"), P())
    return jax.shard_map(
        local,
        mesh=mesh,
        in_specs=placed,
        out_specs=(P("prow", "pcol"), P(None, None, "prow")),
        check_vma=False,
    )
```

```python
import jax
import jax.numpy as jnp
from jax import lax
from jax.experimental import pallas as pl
from jax.experimental.pallas import tpu as pltpu
from jax.sharding import PartitionSpec as P

MESH = pl.DeviceIdType.MESH
F32, BF16 = jnp.float32, jnp.bfloat16
NT = (((1,), (1,)), ((), ()))


def split(x):
    hi = x.astype(BF16)
    return hi, (x - hi.astype(F32)).astype(BF16)


def kernel(umap, sig_in, l_in, c_out, g_out, sig, l_ref, lhi, llo, fs, rc, stf, bhi, blo, lx, lb, ahi, alo, prod, xr, zr, fin, leg, got, dsend, dr, g,
           in_s, out_s, zs_s, zs_r, cs_s, cs_r, lx_s, lx_r, l_s, f_s, o_s, l_r, x_s, x_r, z_s, z_r, a_s, a_r, b_s, b_r, d_s, d_r, g_s, g_r):
    me_r, me_c = lax.axis_index("prow"), lax.axis_index("pcol")
    y, xh = me_r // 2, me_r % 2
    half, j = me_c // 8, me_c % 8
    zl, xl, k = j // 4, (j // 2) % 2, j % 2
    chunks, width = fs.shape[0], fs.shape[1]
    tile = sig.shape[1]
    tiles = 2 * chunks
    rows = l_ref.shape[0]
    part = rows // 4
    steps = 4 * chunks

    def dev(y_, xh_, zl_, xl_, k_):
        return (y_ * 2 + xh_, half * 8 + zl_ * 4 + xl_ * 2 + k_)

    partner = (me_r, (me_c + 8) % 16)
    other_core = dev(y, xh, zl, xl, 1 - k)

    def copy(src, dst, ssem, rsem, to):
        return pltpu.make_async_remote_copy(
            src_ref=src, dst_ref=dst, send_sem=ssem, recv_sem=rsem, device_id=to, device_id_type=MESH)

    load_l = pltpu.make_async_copy(l_in, l_ref, in_s.at[0])
    load_sig = pltpu.make_async_copy(sig_in, sig, in_s.at[1])
    load_l.start()
    load_sig.start()

    barrier = pltpu.get_barrier_semaphore()

    def greet(to):
        pl.semaphore_signal(barrier, inc=1, device_id=to, device_id_type=MESH)

    for d in range(1, 16):
        greet((me_r, (me_c + d) % 16))
    for d in range(1, 4):
        for kk in range(2):
            greet(dev((y + d) % 4, xh, zl, xl, kk))
    for d in range(8):
        greet((2 * y + 1 - xh, half * 8 + d))
    pl.semaphore_wait(barrier, 29)

    def cross():
        return copy(l_ref, lx, lx_s, lx_r, dev(y, 1 - xh, zl, xl, k))

    def spread(src, core, sems, d):
        return copy(src, lb.at[y, k], sems.at[d], l_r.at[y, k], dev((y + d) % 4, xh, zl, xl, core))

    def spread_start(src, core, sems):
        for d in (1, 3):
            spread(src, core, sems, d).start()

        @pl.when(k != core)
        def _():
            spread(src, core, sems, 0).start()

        @pl.when(k == core)
        def _():
            pltpu.make_async_copy(src, lb.at[y, core], l_r.at[y, core]).start()

    def spread_end(src, core, sems):
        for d in (1, 3):
            spread(src, core, sems, d).wait_send()

        @pl.when(k != core)
        def _():
            spread(src, core, sems, 0).wait_send()

    def onward(t):
        yf, yt, kk = (y + 1 + 2 * (t - 1)) % 4, (y + 3 - 2 * (t - 1)) % 4, 2 - t
        return copy(lb.at[yf, kk], lb.at[yf, kk], o_s.at[t - 1], l_r.at[yf, kk], dev(yt, xh, zl, xl, k))

    load_l.wait()
    def arrived(yf, kk):
        copy(lb.at[yf, kk], lb.at[yf, kk], l_s.at[0], l_r.at[yf, kk], other_core).wait_recv()

    cross().start()
    spread_start(l_ref, 0, l_s)

    def far_copy(q):
        return copy(fs.at[q], rc.at[q], zs_s.at[q], zs_r.at[q], partner)

    load_sig.wait()
    for q in range(chunks):
        for h in range(2):
            row = umap[1 - half, me_r * tiles + 2 * q + h] // 8
            fs[q, h * tile:(h + 1) * tile, :] = sig[row]
        far_copy(q).start()
    hi, lo = split(l_ref[...])
    lhi[...] = hi
    llo[...] = lo

    def core_copy(kk, q):
        return copy(stf.at[kk, q], stf.at[kk, q], cs_s.at[q], cs_r.at[q], other_core)

    def take_s(q):
        far_copy(q).wait_recv()
        for h in range(2):
            row = umap[half, me_r * tiles + 2 * q + h] // 8
            near = sig[row]
            far = rc[q, h * tile:(h + 1) * tile, :]
            for s in range(tiles):
                col = umap[half, j * tiles + s]
                spot = col // 16 + tiles * (((col // 8) % 2 + half) % 2)
                x = near[:, :tile]
                for c in range(1, 2 * tiles):
                    lanes = slice((c % tiles) * tile, (c % tiles + 1) * tile)
                    x = jnp.where(spot == c, (near if c < tiles else far)[:, lanes], x)
                stf[k, q, s * tile:(s + 1) * tile, h * tile:(h + 1) * tile] = x.T
        core_copy(k, q).start()
        hi, lo = split(stf[k, q])
        bhi[q, k] = hi
        blo[q, k] = lo
        core_copy(1 - k, q).wait_recv()
        hi, lo = split(stf[1 - k, q])
        bhi[q, 1 - k] = hi
        blo[q, 1 - k] = lo

    def where_of(n):
        last = n // (3 * chunks)
        t = (1 - k) * ((1 - last) * (n % 3) + last * 3) + k * (n // chunks)
        q = (1 - k) * ((1 - last) * (n // 3) + last * (n - 3 * chunks)) + k * (n % chunks)
        return t, q, t + (t // 2) * (1 - 2 * (t % 2))

    def order(t, q):
        f = (q // (chunks - 1)) * (t // 2)
        return f, f * zl + (1 - f) * xl, f * xl + (1 - f) * zl

    def peer(f):
        return dev(y, xh, zl + f * (1 - 2 * zl), xl + (1 - f) * (1 - 2 * xl), k)

    def x_copy(t, q):
        f, b1, _ = order(t, q)
        return copy(prod.at[t, q, pl.ds(2 * part * (1 - b1), 2 * part)], xr.at[t, q], x_s.at[t, q], x_r.at[t, q], peer(f))

    def z_copy(t, q):
        f, _, b2 = order(t, q)
        return copy(xr.at[t, q, pl.ds(part * (1 - b2), part)], zr.at[t, q], z_s.at[t, q], z_r.at[t, q], peer(1 - f))

    def spot_of(t, q):
        _, b1, b2 = order(t, q)
        return pl.ds(2 * part * b1 + part * b2, part)

    def a_copy(t, q, dy):
        return copy(fin.at[t, q], leg.at[y, q], a_s.at[t, q], a_r.at[y, q], dev((y + dy) % 4, xh, zl, xl, k))

    def t_of(ys):
        dy = (y + 4 - ys) % 4
        return dy + (dy // 2) * (1 - 2 * (dy % 2))

    def b_copy(ys, q):
        t = t_of(ys)
        _, b1, b2 = order(t, q)
        to = dev(y, (xh + k) % 2, ys // 2, ys % 2, xh)
        return copy(leg.at[ys, q], got.at[q, spot_of(t, q)], b_s.at[ys, q], b_r.at[q, b1, b2], to)

    def b_stays(ys):
        return (ys == 2 * zl + xl) & (xh == 0) & (k == 0)

    lag_x, lag_z, lag_a = 2, 4, 8

    def x_stage(n, carry):
        t, q, _ = where_of(n)
        _, b1, _ = order(t, q)
        x_copy(t, q).wait_recv()
        xr[t, q] = xr[t, q] + prod[t, q, pl.ds(2 * part * b1, 2 * part)]
        z_copy(t, q).start()
        return carry

    def z_stage(n, carry):
        t, q, dy = where_of(n)
        _, _, b2 = order(t, q)
        z_copy(t, q).wait_recv()
        done = -(xr[t, q, pl.ds(part * b2, part)] + zr[t, q])

        @pl.when(t == 0)
        def _():
            leg[y, q] = done

        @pl.when(t > 0)
        def _():
            fin[t, q] = done
            a_copy(t, q, dy).start()
        return carry

    def a_stage(n, carry):
        t, q, dy = where_of(n)
        ys = (y + 4 - dy) % 4

        @pl.when(t > 0)
        def _():
            copy(leg.at[ys, q], leg.at[ys, q], a_s.at[0, 0], a_r.at[ys, q], other_core).wait_recv()

        @pl.when(b_stays(ys))
        def _():
            got[q, spot_of(t_of(ys), q)] = leg[ys, q]

        @pl.when(jnp.logical_not(b_stays(ys)))
        def _():
            b_copy(ys, q).start()
        return carry

    def turn(v, carry):
        @pl.when(v < steps)
        def _():
            n = v
            t, q, dy = where_of(n)
            yp = (y + dy) % 4

            @pl.when(t == 0)
            def _():
                take_s(q)

            @pl.when(n == 1 - k)
            def _():
                cross().wait_recv()
                spread_start(lx, 1, f_s)

            @pl.when(q == 0)
            def _():
                arrived(yp, 1)

                @pl.when(t != 2)
                def _():
                    arrived(yp, 0)

                @pl.when(t == 1)
                def _():
                    onward(1).start()
                    arrived((y + 3) % 4, 0)
                    onward(2).start()

                for kk in range(2):
                    hi, lo = split(lb[yp, kk])
                    ahi[t, kk] = hi
                    alo[t, kk] = lo

            total = jnp.zeros((rows, width), F32)
            for kk in range(2):
                total += jnp.dot(ahi[t, kk], bhi[q, kk], preferred_element_type=F32)
                total += jnp.dot(ahi[t, kk], blo[q, kk], preferred_element_type=F32)
                total += jnp.dot(alo[t, kk], bhi[q, kk], preferred_element_type=F32)
            prod[t, q] = total
            x_copy(t, q).start()

        for stage, lag in ((x_stage, lag_x), (z_stage, lag_z), (a_stage, lag_a)):
            @pl.when((v >= lag) & (v < steps + lag))
            def _():
                stage(v - lag, 0)
        return carry

    lax.fori_loop(0, steps + lag_a, turn, 0)

    def write(q):
        return pltpu.make_async_copy(got.at[q], c_out.at[:, pl.ds(q * width, width)], out_s.at[q])

    diag = [jnp.zeros((tile, tile), F32) for _ in range(rows // tile)]
    for q in range(chunks):
        _, b1, b2 = order(t_of(2 * zl + xl), q)
        for u in range(2):
            for v in range(2):
                @pl.when(jnp.logical_not((u == b1) & (v == b2) & (xh == 0) & (k == 0)))
                def _():
                    spot = got.at[q, pl.ds(2 * part * u + part * v, part)]
                    copy(spot, spot, b_s.at[0, 0], b_r.at[q, u, v], other_core).wait_recv()
        cols = slice(q * width, (q + 1) * width)
        write(q).start()
        for t in range(len(diag)):
            span = slice(t * tile, (t + 1) * tile)
            hi, lo = split(got[q, span])
            for left, right in ((hi, lhi), (hi, llo), (lo, lhi)):
                diag[t] += lax.dot_general(left, right[span, cols], NT, preferred_element_type=F32)
    for t in range(len(diag)):
        dsend[:, :, t * tile:(t + 1) * tile] = diag[t].reshape(8, tile // 8, tile)

    def d_copy(d):
        to = (j + d) % 8
        return copy(dsend.at[to], dr.at[j], d_s.at[d], d_r.at[j], (me_r, half * 8 + to))

    def d_from(d):
        frm = (j + d) % 8
        return copy(dsend.at[frm], dr.at[frm], d_s.at[d], d_r.at[frm], (me_r, half * 8 + frm))

    for d in range(1, 8):
        d_copy(d).start()
    cross().wait_send()
    spread_end(l_ref, 0, l_s)
    spread_end(lx, 1, f_s)
    for t in (1, 2):
        onward(t).wait_send()
    for q in range(chunks):
        far_copy(q).wait_send()
        core_copy(k, q).wait_send()

    def sent(n, carry):
        t, q, dy = where_of(n)
        ys = (y + 4 - dy) % 4
        x_copy(t, q).wait_send()
        z_copy(t, q).wait_send()

        @pl.when(t > 0)
        def _():
            a_copy(t, q, dy).wait_send()

        @pl.when(jnp.logical_not(b_stays(ys)))
        def _():
            b_copy(ys, q).wait_send()
        return carry

    lax.fori_loop(0, steps, sent, 0)
    for q in range(chunks):
        write(q).wait()
    dr[j] = dsend[j]
    for d in range(1, 8):
        d_from(d).wait_recv()
    total = dr[0]
    for d in range(1, 8):
        total += dr[d]
    g[me_c] = total

    def g_copy(d):
        return copy(g.at[me_c], g.at[me_c], g_s.at[d], g_r.at[me_c], (me_r, (me_c + 2 * d) % 16))

    def g_from(d):
        frm = (me_c + 2 * d) % 16
        return copy(g.at[frm], g.at[frm], g_s.at[d], g_r.at[frm], (me_r, frm))

    def h_copy(d):
        frm = (me_c + 2 * d) % 16
        return copy(g.at[frm], g.at[frm], g_s.at[8 + d], g_r.at[frm], other_core)

    def h_from(d):
        frm = (me_c + 1 - 2 * k + 2 * d) % 16
        return copy(g.at[frm], g.at[frm], g_s.at[8 + d], g_r.at[frm], other_core)

    for d in range(1, 8):
        g_copy(d).start()
    h_copy(0).start()
    for d in range(1, 8):
        g_from(d).wait_recv()
        h_copy(d).start()
    for d in range(8):
        h_from(d).wait_recv()
    g_out[...] = g[...].reshape(g_out.shape)

    for d in range(1, 8):
        d_copy(d).wait_send()
    for d in range(1, 8):
        g_copy(d).wait_send()
    for d in range(8):
        h_copy(d).wait_send()


def finish(c_ref, g_ref, pd_ref, c_out, m_out):
    c_out[...] = c_ref[...]
    for h in range(2):
        m_out[:, h, :] = pd_ref[:, h, :] - g_ref[h]


def local(root_sigma, pivot_diag, update_l, update_map):
    tile = pivot_diag.shape[0]
    rows, cols = update_l.shape
    chunks = 3
    width = cols // chunks
    sem = pltpu.SemaphoreType.DMA
    vmem = pl.BlockSpec(memory_space=pltpu.VMEM)
    anywhere = pl.BlockSpec(memory_space=pl.ANY)
    product, diagonal = pl.pallas_call(
        kernel,
        out_shape=(jax.ShapeDtypeStruct(update_l.shape, F32), jax.ShapeDtypeStruct((2, tile, rows), F32)),
        in_specs=[pl.BlockSpec(memory_space=pltpu.SMEM), anywhere, anywhere],
        out_specs=(anywhere, vmem),
        scratch_shapes=[
            pltpu.VMEM((root_sigma.shape[0] // tile, tile, root_sigma.shape[1]), F32),
            pltpu.VMEM((rows, cols), F32),
            pltpu.VMEM((rows, cols), BF16),
            pltpu.VMEM((rows, cols), BF16),
            pltpu.VMEM((chunks, width, cols), F32),
            pltpu.VMEM((chunks, width, cols), F32),
            pltpu.VMEM((2, chunks, cols, width), F32),
            pltpu.VMEM((chunks, 2, cols, width), BF16),
            pltpu.VMEM((chunks, 2, cols, width), BF16),
            pltpu.VMEM((rows, cols), F32),
            pltpu.VMEM((4, 2, rows, cols), F32),
            pltpu.VMEM((4, 2, rows, cols), BF16),
            pltpu.VMEM((4, 2, rows, cols), BF16),
            pltpu.VMEM((4, chunks, rows, width), F32),
            pltpu.VMEM((4, chunks, rows // 2, width), F32),
            pltpu.VMEM((4, chunks, rows // 4, width), F32),
            pltpu.VMEM((4, chunks, rows // 4, width), F32),
            pltpu.VMEM((4, chunks, rows // 4, width), F32),
            pltpu.VMEM((chunks, rows, width), F32),
            pltpu.VMEM((8, tile // 8, rows), F32),
            pltpu.VMEM((8, tile // 8, rows), F32),
            pltpu.VMEM((16, tile // 8, rows), F32),
            sem((2,)), sem((chunks,)),
            sem((chunks,)), sem((chunks,)), sem((chunks,)), sem((chunks,)),
            sem, sem, sem((4,)), sem((4,)), sem((2,)), sem((4, 2)),
            sem((4, chunks)), sem((4, chunks)), sem((4, chunks)), sem((4, chunks)),
            sem((4, chunks)), sem((4, chunks)), sem((4, chunks)), sem((chunks, 2, 2)),
            sem((8,)), sem((8,)), sem((16,)), sem((16,)),
        ],
        compiler_params=pltpu.CompilerParams(
            collective_id=0, has_side_effects=True, vmem_limit_bytes=62 * 2**20),
        name="selected_inverse",
    )(update_map, root_sigma.reshape(-1, tile, root_sigma.shape[1]), update_l)
    return pl.pallas_call(
        finish,
        out_shape=(jax.ShapeDtypeStruct(update_l.shape, F32), jax.ShapeDtypeStruct(pivot_diag.shape, F32)),
        in_specs=[vmem, vmem, vmem],
        out_specs=(vmem, vmem),
        name="write_results",
    )(product, diagonal, pivot_diag)


def solution(mesh):
    placed = (P("prow", "pcol"), P(None, None, "prow"), P("prow", "pcol"), P())
    return jax.shard_map(
        local,
        mesh=mesh,
        in_specs=placed,
        out_specs=(P("prow", "pcol"), P(None, None, "prow")),
        check_vma=False,
    )
```

```python
import jax
import jax.numpy as jnp
from jax import lax
from jax.experimental import pallas as pl
from jax.experimental.pallas import tpu as pltpu
from jax.sharding import PartitionSpec as P

MESH = pl.DeviceIdType.MESH
F32, BF16 = jnp.float32, jnp.bfloat16
NT = (((1,), (1,)), ((), ()))


def split(x):
    hi = x.astype(BF16)
    return hi, (x - hi.astype(F32)).astype(BF16)


def kernel(umap, sig_in, l_in, c_out, g_out, sig, l_ref, lhi, llo, fs, rc, stf, bhi, blo, lx, lb, ahi, alo, prod, xr, zr, fin, leg, got, dsend, dr, summed,
           in_s, out_s, zs_s, zs_r, cs_s, cs_r, lx_s, lx_r, l_s, f_s, o_s, l_r, x_s, x_r, z_s, z_r, a_s, a_r, b_s, b_r, d_s, d_r, g_s, g_r):
    me_r, me_c = lax.axis_index("prow"), lax.axis_index("pcol")
    y, xh = me_r // 2, me_r % 2
    half, j = me_c // 8, me_c % 8
    zl, xl, k = j // 4, (j // 2) % 2, j % 2
    chunks, width = fs.shape[0], fs.shape[1]
    tile = sig.shape[1]
    tiles = 2 * chunks
    rows = l_ref.shape[0]
    part = rows // 4
    steps = 4 * chunks

    def dev(y_, xh_, zl_, xl_, k_):
        return (y_ * 2 + xh_, half * 8 + zl_ * 4 + xl_ * 2 + k_)

    partner = (me_r, (me_c + 8) % 16)
    other_core = dev(y, xh, zl, xl, 1 - k)

    def copy(src, dst, ssem, rsem, to):
        return pltpu.make_async_remote_copy(
            src_ref=src, dst_ref=dst, send_sem=ssem, recv_sem=rsem, device_id=to, device_id_type=MESH)

    load_l = pltpu.make_async_copy(l_in, l_ref, in_s.at[0])
    load_sig = pltpu.make_async_copy(sig_in, sig, in_s.at[1])
    load_l.start()
    load_sig.start()

    barrier = pltpu.get_barrier_semaphore()

    def greet(to):
        pl.semaphore_signal(barrier, inc=1, device_id=to, device_id_type=MESH)

    greet(dev(y, 1 - xh, zl, xl, k))
    for d in (1, 3):
        for kk in range(2):
            greet(dev((y + d) % 4, xh, zl, xl, kk))
    greet(dev((y + 2) % 4, xh, zl, xl, k))
    for d in range(1, 8):
        greet((me_r, half * 8 + (j + d) % 8))
    for d in range(4):
        greet((me_r, (1 - half) * 8 + 2 * d + k))

    @pl.when(k == 1 - xh)
    def _():
        for d in range(4):
            greet((2 * y + 1 - xh, half * 8 + 2 * d + 1))

    pl.semaphore_wait(barrier, 17 + 4 * k)

    def cross():
        return copy(l_ref, lx, lx_s, lx_r, dev(y, 1 - xh, zl, xl, k))

    def spread(src, core, sems, d):
        return copy(src, lb.at[y, k], sems.at[d], l_r.at[y, k], dev((y + d) % 4, xh, zl, xl, core))

    def spread_start(src, core, sems):
        for d in (1, 3):
            spread(src, core, sems, d).start()

        @pl.when(k != core)
        def _():
            spread(src, core, sems, 0).start()

        @pl.when(k == core)
        def _():
            pltpu.make_async_copy(src, lb.at[y, core], l_r.at[y, core]).start()

    def spread_end(src, core, sems):
        for d in (1, 3):
            spread(src, core, sems, d).wait_send()

        @pl.when(k != core)
        def _():
            spread(src, core, sems, 0).wait_send()

    def onward(t):
        yf, yt, kk = (y + 1 + 2 * (t - 1)) % 4, (y + 3 - 2 * (t - 1)) % 4, 2 - t
        return copy(lb.at[yf, kk], lb.at[yf, kk], o_s.at[t - 1], l_r.at[yf, kk], dev(yt, xh, zl, xl, k))

    load_l.wait()
    def arrived(yf, kk):
        copy(lb.at[yf, kk], lb.at[yf, kk], l_s.at[0], l_r.at[yf, kk], other_core).wait_recv()

    cross().start()
    spread_start(l_ref, 0, l_s)

    def far_copy(q):
        return copy(fs.at[q], rc.at[q], zs_s.at[q], zs_r.at[q], partner)

    load_sig.wait()
    for q in range(chunks):
        for h in range(2):
            row = umap[1 - half, me_r * tiles + 2 * q + h] // 8
            fs[q, h * tile:(h + 1) * tile, :] = sig[row]
        far_copy(q).start()
    hi, lo = split(l_ref[...])
    lhi[...] = hi
    llo[...] = lo

    def core_copy(kk, q):
        return copy(stf.at[kk, q], stf.at[kk, q], cs_s.at[q], cs_r.at[q], other_core)

    def take_s(q):
        far_copy(q).wait_recv()
        for h in range(2):
            row = umap[half, me_r * tiles + 2 * q + h] // 8
            near = sig[row]
            far = rc[q, h * tile:(h + 1) * tile, :]
            for s in range(tiles):
                col = umap[half, j * tiles + s]
                spot = col // 16 + tiles * (((col // 8) % 2 + half) % 2)
                x = near[:, :tile]
                for c in range(1, 2 * tiles):
                    lanes = slice((c % tiles) * tile, (c % tiles + 1) * tile)
                    x = jnp.where(spot == c, (near if c < tiles else far)[:, lanes], x)
                stf[k, q, s * tile:(s + 1) * tile, h * tile:(h + 1) * tile] = x.T
        core_copy(k, q).start()
        hi, lo = split(stf[k, q])
        bhi[q, k] = hi
        blo[q, k] = lo
        core_copy(1 - k, q).wait_recv()
        hi, lo = split(stf[1 - k, q])
        bhi[q, 1 - k] = hi
        blo[q, 1 - k] = lo

    def where_of(n):
        last = n // (3 * chunks)
        t = (1 - k) * ((1 - last) * (n % 3) + last * 3) + k * (n // chunks)
        q = (1 - k) * ((1 - last) * (n // 3) + last * (n - 3 * chunks)) + k * (n % chunks)
        return t, q, t + (t // 2) * (1 - 2 * (t % 2))

    def order(t, q):
        f = (q // (chunks - 1)) * (t // 2)
        return f, f * zl + (1 - f) * xl, f * xl + (1 - f) * zl

    def peer(f):
        return dev(y, xh, zl + f * (1 - 2 * zl), xl + (1 - f) * (1 - 2 * xl), k)

    def x_copy(t, q):
        f, b1, _ = order(t, q)
        return copy(prod.at[t, q, pl.ds(2 * part * (1 - b1), 2 * part)], xr.at[t, q], x_s.at[t, q], x_r.at[t, q], peer(f))

    def z_copy(t, q):
        f, _, b2 = order(t, q)
        return copy(xr.at[t, q, pl.ds(part * (1 - b2), part)], zr.at[t, q], z_s.at[t, q], z_r.at[t, q], peer(1 - f))

    def spot_of(t, q):
        _, b1, b2 = order(t, q)
        return pl.ds(2 * part * b1 + part * b2, part)

    def a_copy(t, q, dy):
        return copy(fin.at[t, q], leg.at[y, q], a_s.at[t, q], a_r.at[y, q], dev((y + dy) % 4, xh, zl, xl, k))

    def t_of(ys):
        dy = (y + 4 - ys) % 4
        return dy + (dy // 2) * (1 - 2 * (dy % 2))

    def b_copy(ys, q):
        t = t_of(ys)
        _, b1, b2 = order(t, q)
        to = dev(y, (xh + k) % 2, ys // 2, ys % 2, xh)
        return copy(leg.at[ys, q], got.at[q, spot_of(t, q)], b_s.at[ys, q], b_r.at[q, b1, b2], to)

    def b_stays(ys):
        return (ys == 2 * zl + xl) & (xh == 0) & (k == 0)

    lag_x, lag_z, lag_a = 2, 4, 8

    def x_stage(n, carry):
        t, q, _ = where_of(n)
        _, b1, _ = order(t, q)
        x_copy(t, q).wait_recv()
        xr[t, q] = xr[t, q] + prod[t, q, pl.ds(2 * part * b1, 2 * part)]
        z_copy(t, q).start()
        return carry

    def z_stage(n, carry):
        t, q, dy = where_of(n)
        _, _, b2 = order(t, q)
        z_copy(t, q).wait_recv()
        done = -(xr[t, q, pl.ds(part * b2, part)] + zr[t, q])

        @pl.when(t == 0)
        def _():
            leg[y, q] = done

        @pl.when(t > 0)
        def _():
            fin[t, q] = done
            a_copy(t, q, dy).start()
        return carry

    def a_stage(n, carry):
        t, q, dy = where_of(n)
        ys = (y + 4 - dy) % 4

        @pl.when(t > 0)
        def _():
            copy(leg.at[ys, q], leg.at[ys, q], a_s.at[0, 0], a_r.at[ys, q], other_core).wait_recv()

        @pl.when(b_stays(ys))
        def _():
            got[q, spot_of(t_of(ys), q)] = leg[ys, q]

        @pl.when(jnp.logical_not(b_stays(ys)))
        def _():
            b_copy(ys, q).start()
        return carry

    def turn(v, carry):
        @pl.when(v < steps)
        def _():
            n = v
            t, q, dy = where_of(n)
            yp = (y + dy) % 4

            @pl.when(t == 0)
            def _():
                take_s(q)

            @pl.when(n == 1 - k)
            def _():
                cross().wait_recv()
                spread_start(lx, 1, f_s)

            @pl.when(q == 0)
            def _():
                arrived(yp, 1)

                @pl.when(t != 2)
                def _():
                    arrived(yp, 0)

                @pl.when(t == 1)
                def _():
                    onward(1).start()
                    arrived((y + 3) % 4, 0)
                    onward(2).start()

                for kk in range(2):
                    hi, lo = split(lb[yp, kk])
                    ahi[t, kk] = hi
                    alo[t, kk] = lo

            total = jnp.zeros((rows, width), F32)
            for kk in range(2):
                total += jnp.dot(ahi[t, kk], bhi[q, kk], preferred_element_type=F32)
                total += jnp.dot(ahi[t, kk], blo[q, kk], preferred_element_type=F32)
                total += jnp.dot(alo[t, kk], bhi[q, kk], preferred_element_type=F32)
            prod[t, q] = total
            x_copy(t, q).start()

        for stage, lag in ((x_stage, lag_x), (z_stage, lag_z), (a_stage, lag_a)):
            @pl.when((v >= lag) & (v < steps + lag))
            def _():
                stage(v - lag, 0)
        return carry

    lax.fori_loop(0, steps + lag_a, turn, 0)

    def write(q):
        return pltpu.make_async_copy(got.at[q], c_out.at[:, pl.ds(q * width, width)], out_s.at[q])

    diag = [jnp.zeros((tile, tile), F32) for _ in range(rows // tile)]
    for q in range(chunks):
        _, b1, b2 = order(t_of(2 * zl + xl), q)
        for u in range(2):
            for v in range(2):
                @pl.when(jnp.logical_not((u == b1) & (v == b2) & (xh == 0) & (k == 0)))
                def _():
                    spot = got.at[q, pl.ds(2 * part * u + part * v, part)]
                    copy(spot, spot, b_s.at[0, 0], b_r.at[q, u, v], other_core).wait_recv()
        cols = slice(q * width, (q + 1) * width)
        write(q).start()
        for t in range(len(diag)):
            span = slice(t * tile, (t + 1) * tile)
            hi, lo = split(got[q, span])
            for left, right in ((hi, lhi), (hi, llo), (lo, lhi)):
                diag[t] += lax.dot_general(left, right[span, cols], NT, preferred_element_type=F32)
    for t in range(len(diag)):
        dsend[:, :, t * tile:(t + 1) * tile] = diag[t].reshape(8, tile // 8, tile)

    def d_copy(d):
        to = (j + d) % 8
        return copy(dsend.at[to], dr.at[j], d_s.at[d], d_r.at[j], (me_r, half * 8 + to))

    def d_from(d):
        frm = (j + d) % 8
        return copy(dsend.at[frm], dr.at[frm], d_s.at[d], d_r.at[frm], (me_r, half * 8 + frm))

    for d in range(1, 8):
        d_copy(d).start()
    cross().wait_send()
    spread_end(l_ref, 0, l_s)
    spread_end(lx, 1, f_s)
    for t in (1, 2):
        onward(t).wait_send()
    for q in range(chunks):
        far_copy(q).wait_send()
        core_copy(k, q).wait_send()

    def sent(n, carry):
        t, q, dy = where_of(n)
        ys = (y + 4 - dy) % 4
        x_copy(t, q).wait_send()
        z_copy(t, q).wait_send()

        @pl.when(t > 0)
        def _():
            a_copy(t, q, dy).wait_send()

        @pl.when(jnp.logical_not(b_stays(ys)))
        def _():
            b_copy(ys, q).wait_send()
        return carry

    lax.fori_loop(0, steps, sent, 0)
    for q in range(chunks):
        write(q).wait()
    dr[j] = dsend[j]
    for d in range(1, 8):
        d_from(d).wait_recv()
    total = dr[0]
    for d in range(1, 8):
        total += dr[d]
    summed[...] = total

    stay_g = pltpu.make_async_copy(summed, g_out.at[me_c], g_r.at[me_c])

    def g_copy(d):
        return copy(summed, g_out.at[me_c], g_s.at[d], g_r.at[me_c], (me_r, (me_c + 2 * d) % 16))

    def g_from(d):
        frm = (me_c + 2 * d) % 16
        return copy(summed, g_out.at[frm], g_s.at[d], g_r.at[frm], (me_r, frm))

    def h_copy(d):
        frm = (me_c + 2 * d) % 16
        src = summed if d == 0 else g_out.at[frm]
        return copy(src, g_out.at[frm], g_s.at[8 + d], g_r.at[frm], other_core)

    def h_from(d):
        frm = (me_c + 1 - 2 * k + 2 * d) % 16
        return copy(summed, g_out.at[frm], g_s.at[8 + d], g_r.at[frm], other_core)

    for d in range(1, 8):
        g_copy(d).start()
    h_copy(0).start()
    stay_g.start()
    for d in range(1, 8):
        g_from(d).wait_recv()
        h_copy(d).start()
    for d in range(8):
        h_from(d).wait_recv()
    stay_g.wait()

    for d in range(1, 8):
        d_copy(d).wait_send()
    for d in range(1, 8):
        g_copy(d).wait_send()
    for d in range(8):
        h_copy(d).wait_send()


def finish(c_ref, g_ref, pd_ref, c_out, m_out):
    c_out[...] = c_ref[...]
    for h in range(2):
        m_out[:, h, :] = pd_ref[:, h, :] - g_ref[h]


def local(root_sigma, pivot_diag, update_l, update_map):
    tile = pivot_diag.shape[0]
    rows, cols = update_l.shape
    chunks, parts = 3, 2
    width = cols // chunks
    sem = pltpu.SemaphoreType.DMA
    vmem = pl.BlockSpec(memory_space=pltpu.VMEM)
    anywhere = pl.BlockSpec(memory_space=pl.ANY)
    product, diagonal = pl.pallas_call(
        kernel,
        out_shape=(jax.ShapeDtypeStruct(update_l.shape, F32), jax.ShapeDtypeStruct((16, tile // 8, rows), F32)),
        in_specs=[pl.BlockSpec(memory_space=pltpu.SMEM), anywhere, anywhere],
        out_specs=(anywhere, anywhere),
        scratch_shapes=[
            pltpu.VMEM((root_sigma.shape[0] // tile, tile, root_sigma.shape[1]), F32),
            pltpu.VMEM((rows, cols), F32),
            pltpu.VMEM((rows, cols), BF16),
            pltpu.VMEM((rows, cols), BF16),
            pltpu.VMEM((chunks, width, cols), F32),
            pltpu.VMEM((chunks, width, cols), F32),
            pltpu.VMEM((2, chunks, cols, width), F32),
            pltpu.VMEM((chunks, 2, cols, width), BF16),
            pltpu.VMEM((chunks, 2, cols, width), BF16),
            pltpu.VMEM((rows, cols), F32),
            pltpu.VMEM((4, 2, rows, cols), F32),
            pltpu.VMEM((4, 2, rows, cols), BF16),
            pltpu.VMEM((4, 2, rows, cols), BF16),
            pltpu.VMEM((4, chunks, rows, width), F32),
            pltpu.VMEM((4, chunks, rows // 2, width), F32),
            pltpu.VMEM((4, chunks, rows // 4, width), F32),
            pltpu.VMEM((4, chunks, rows // 4, width), F32),
            pltpu.VMEM((4, chunks, rows // 4, width), F32),
            pltpu.VMEM((chunks, rows, width), F32),
            pltpu.VMEM((8, tile // 8, rows), F32),
            pltpu.VMEM((8, tile // 8, rows), F32),
            pltpu.VMEM((tile // 8, rows), F32),
            sem((2,)), sem((chunks,)),
            sem((chunks,)), sem((chunks,)), sem((chunks,)), sem((chunks,)),
            sem, sem, sem((4,)), sem((4,)), sem((2,)), sem((4, 2)),
            sem((4, chunks)), sem((4, chunks)), sem((4, chunks)), sem((4, chunks)),
            sem((4, chunks)), sem((4, chunks)), sem((4, chunks)), sem((chunks, 2, 2)),
            sem((8,)), sem((8,)), sem((16,)), sem((16,)),
        ],
        compiler_params=pltpu.CompilerParams(
            collective_id=0, has_side_effects=True, vmem_limit_bytes=62 * 2**20),
        name="selected_inverse",
    )(update_map, root_sigma.reshape(-1, tile, root_sigma.shape[1]), update_l)
    return pl.pallas_call(
        finish,
        out_shape=(jax.ShapeDtypeStruct(update_l.shape, F32), jax.ShapeDtypeStruct(pivot_diag.shape, F32)),
        grid=(parts,),
        in_specs=[
            pl.BlockSpec((rows // parts, cols), lambda n: (n, 0)),
            pl.BlockSpec((2, tile // parts, rows), lambda n: (0, n, 0)),
            pl.BlockSpec((tile // parts, 2, rows), lambda n: (n, 0, 0)),
        ],
        out_specs=(
            pl.BlockSpec((rows // parts, cols), lambda n: (n, 0)),
            pl.BlockSpec((tile // parts, 2, rows), lambda n: (n, 0, 0)),
        ),
        name="write_results",
    )(product, diagonal.reshape(2, tile, rows), pivot_diag)


def solution(mesh):
    placed = (P("prow", "pcol"), P(None, None, "prow"), P("prow", "pcol"), P())
    return jax.shard_map(
        local,
        mesh=mesh,
        in_specs=placed,
        out_specs=(P("prow", "pcol"), P(None, None, "prow")),
        check_vma=False,
    )
```

```python
import jax
import jax.numpy as jnp
from jax import lax
from jax.experimental import pallas as pl
from jax.experimental.pallas import tpu as pltpu
from jax.sharding import PartitionSpec as P

MESH = pl.DeviceIdType.MESH
F32, BF16 = jnp.float32, jnp.bfloat16
NT = (((1,), (1,)), ((), ()))


def split(x):
    hi = x.astype(BF16)
    return hi, (x - hi.astype(F32)).astype(BF16)


def kernel(umap, sig_in, l_in, c_out, g_out, sig, l_ref, lhi, llo, fs, rc, stf, bhi, blo, lx, lb, ahi, alo, prod, xr, zr, fin, leg, got, dsend, dr, summed,
           in_s, out_s, zs_s, zs_r, cs_s, cs_r, lx_s, lx_r, l_s, f_s, o_s, l_r, x_s, x_r, z_s, z_r, a_s, a_r, b_s, b_r, d_s, d_r, g_s, g_r):
    me_r, me_c = lax.axis_index("prow"), lax.axis_index("pcol")
    y, xh = me_r // 2, me_r % 2
    half, j = me_c // 8, me_c % 8
    zl, xl, k = j // 4, (j // 2) % 2, j % 2
    chunks, width = fs.shape[0], fs.shape[1]
    tile = sig.shape[1]
    tiles = 2 * chunks
    rows = l_ref.shape[0]
    part = rows // 4
    steps = 4 * chunks

    def dev(y_, xh_, zl_, xl_, k_):
        return (y_ * 2 + xh_, half * 8 + zl_ * 4 + xl_ * 2 + k_)

    partner = (me_r, (me_c + 8) % 16)
    other_core = dev(y, xh, zl, xl, 1 - k)

    def copy(src, dst, ssem, rsem, to):
        return pltpu.make_async_remote_copy(
            src_ref=src, dst_ref=dst, send_sem=ssem, recv_sem=rsem, device_id=to, device_id_type=MESH)

    load_l = pltpu.make_async_copy(l_in, l_ref, in_s.at[0])
    load_sig = pltpu.make_async_copy(sig_in, sig, in_s.at[1])
    load_l.start()
    load_sig.start()

    barrier = pltpu.get_barrier_semaphore()

    def greet(to):
        pl.semaphore_signal(barrier, inc=1, device_id=to, device_id_type=MESH)

    greet(dev(y, 1 - xh, zl, xl, k))
    for d in (1, 3):
        for kk in range(2):
            greet(dev((y + d) % 4, xh, zl, xl, kk))
    greet(dev((y + 2) % 4, xh, zl, xl, k))
    for d in range(1, 8):
        greet((me_r, half * 8 + (j + d) % 8))
    for d in range(4):
        greet((me_r, (1 - half) * 8 + 2 * d + k))

    @pl.when(k == 1 - xh)
    def _():
        for d in range(4):
            greet((2 * y + 1 - xh, half * 8 + 2 * d + 1))

    pl.semaphore_wait(barrier, 17 + 4 * k)

    def cross():
        return copy(l_ref, lx, lx_s, lx_r, dev(y, 1 - xh, zl, xl, k))

    def spread(src, core, sems, d):
        return copy(src, lb.at[y, k], sems.at[d], l_r.at[y, k], dev((y + d) % 4, xh, zl, xl, core))

    def spread_start(src, core, sems):
        for d in (1, 3):
            spread(src, core, sems, d).start()

        @pl.when(k != core)
        def _():
            spread(src, core, sems, 0).start()

        @pl.when(k == core)
        def _():
            pltpu.make_async_copy(src, lb.at[y, core], l_r.at[y, core]).start()

    def spread_end(src, core, sems):
        for d in (1, 3):
            spread(src, core, sems, d).wait_send()

        @pl.when(k != core)
        def _():
            spread(src, core, sems, 0).wait_send()

    def onward(t):
        yf, yt, kk = (y + 1 + 2 * (t - 1)) % 4, (y + 3 - 2 * (t - 1)) % 4, 2 - t
        return copy(lb.at[yf, kk], lb.at[yf, kk], o_s.at[t - 1], l_r.at[yf, kk], dev(yt, xh, zl, xl, k))

    load_l.wait()
    def arrived(yf, kk):
        copy(lb.at[yf, kk], lb.at[yf, kk], l_s.at[0], l_r.at[yf, kk], other_core).wait_recv()

    cross().start()
    spread_start(l_ref, 0, l_s)

    def far_copy(q):
        return copy(fs.at[q], rc.at[q], zs_s.at[q], zs_r.at[q], partner)

    load_sig.wait()
    for q in range(chunks):
        for h in range(2):
            row = umap[1 - half, me_r * tiles + 2 * q + h] // 8
            fs[q, h * tile:(h + 1) * tile, :] = sig[row]
        far_copy(q).start()
    hi, lo = split(l_ref[...])
    lhi[...] = hi
    llo[...] = lo

    def core_copy(kk, q):
        return copy(stf.at[kk, q], stf.at[kk, q], cs_s.at[q], cs_r.at[q], other_core)

    def take_s(q):
        far_copy(q).wait_recv()
        for h in range(2):
            row = umap[half, me_r * tiles + 2 * q + h] // 8
            near = sig[row]
            far = rc[q, h * tile:(h + 1) * tile, :]
            for s in range(tiles):
                col = umap[half, j * tiles + s]
                spot = col // 16 + tiles * (((col // 8) % 2 + half) % 2)
                x = near[:, :tile]
                for c in range(1, 2 * tiles):
                    lanes = slice((c % tiles) * tile, (c % tiles + 1) * tile)
                    x = jnp.where(spot == c, (near if c < tiles else far)[:, lanes], x)
                stf[k, q, s * tile:(s + 1) * tile, h * tile:(h + 1) * tile] = x.T
        core_copy(k, q).start()
        hi, lo = split(stf[k, q])
        bhi[q, k] = hi
        blo[q, k] = lo
        core_copy(1 - k, q).wait_recv()
        hi, lo = split(stf[1 - k, q])
        bhi[q, 1 - k] = hi
        blo[q, 1 - k] = lo

    def where_of(n):
        last = n // (3 * chunks)
        t = (1 - k) * ((1 - last) * (n % 3) + last * 3) + k * (n // chunks)
        q = (1 - k) * ((1 - last) * (n // 3) + last * (n - 3 * chunks)) + k * (n % chunks)
        return t, q, t + (t // 2) * (1 - 2 * (t % 2))

    def order(t, q):
        f = (q // (chunks - 1)) * (t // 2)
        return f, f * zl + (1 - f) * xl, f * xl + (1 - f) * zl

    def peer(f):
        return dev(y, xh, zl + f * (1 - 2 * zl), xl + (1 - f) * (1 - 2 * xl), k)

    def x_copy(t, q):
        f, b1, _ = order(t, q)
        return copy(prod.at[t, q, pl.ds(2 * part * (1 - b1), 2 * part)], xr.at[t, q], x_s.at[t, q], x_r.at[t, q], peer(f))

    def z_copy(t, q):
        f, _, b2 = order(t, q)
        return copy(xr.at[t, q, pl.ds(part * (1 - b2), part)], zr.at[t, q], z_s.at[t, q], z_r.at[t, q], peer(1 - f))

    def spot_of(t, q):
        _, b1, b2 = order(t, q)
        return pl.ds(2 * part * b1 + part * b2, part)

    def a_copy(t, q, dy):
        return copy(fin.at[t, q], leg.at[y, q], a_s.at[t, q], a_r.at[y, q], dev((y + dy) % 4, xh, zl, xl, k))

    def t_of(ys):
        dy = (y + 4 - ys) % 4
        return dy + (dy // 2) * (1 - 2 * (dy % 2))

    def b_copy(ys, q):
        t = t_of(ys)
        _, b1, b2 = order(t, q)
        to = dev(y, (xh + k) % 2, ys // 2, ys % 2, xh)
        return copy(leg.at[ys, q], got.at[q, spot_of(t, q)], b_s.at[ys, q], b_r.at[q, b1, b2], to)

    def b_stays(ys):
        return (ys == 2 * zl + xl) & (xh == 0) & (k == 0)

    lag_x, lag_z, lag_a = 2, 4, 8

    def x_stage(n, carry):
        t, q, _ = where_of(n)
        _, b1, b2 = order(t, q)
        x_copy(t, q).wait_recv()

        def add(b):
            at = pl.ds(part * b, part)
            xr[t, q, at] = xr[t, q, at] + prod[t, q, pl.ds(2 * part * b1 + part * b, part)]

        add(1 - b2)
        z_copy(t, q).start()
        add(b2)
        return carry

    def z_stage(n, carry):
        t, q, dy = where_of(n)
        _, _, b2 = order(t, q)
        z_copy(t, q).wait_recv()
        done = -(xr[t, q, pl.ds(part * b2, part)] + zr[t, q])

        @pl.when(t == 0)
        def _():
            leg[y, q] = done

        @pl.when(t > 0)
        def _():
            fin[t, q] = done
            a_copy(t, q, dy).start()
        return carry

    def a_stage(n, carry):
        t, q, dy = where_of(n)
        ys = (y + 4 - dy) % 4

        @pl.when(t > 0)
        def _():
            copy(leg.at[ys, q], leg.at[ys, q], a_s.at[0, 0], a_r.at[ys, q], other_core).wait_recv()

        @pl.when(b_stays(ys))
        def _():
            got[q, spot_of(t_of(ys), q)] = leg[ys, q]

        @pl.when(jnp.logical_not(b_stays(ys)))
        def _():
            b_copy(ys, q).start()
        return carry

    def turn(v, carry):
        @pl.when(v < steps)
        def _():
            n = v
            t, q, dy = where_of(n)
            yp = (y + dy) % 4

            @pl.when(t == 0)
            def _():
                take_s(q)

            @pl.when(n == 1 - k)
            def _():
                cross().wait_recv()
                spread_start(lx, 1, f_s)

            @pl.when(q == 0)
            def _():
                arrived(yp, 1)

                @pl.when(t != 2)
                def _():
                    arrived(yp, 0)

                @pl.when(t == 1)
                def _():
                    onward(1).start()
                    arrived((y + 3) % 4, 0)
                    onward(2).start()

                for kk in range(2):
                    hi, lo = split(lb[yp, kk])
                    ahi[t, kk] = hi
                    alo[t, kk] = lo

            total = jnp.zeros((rows, width), F32)
            for kk in range(2):
                total += jnp.dot(ahi[t, kk], bhi[q, kk], preferred_element_type=F32)
                total += jnp.dot(ahi[t, kk], blo[q, kk], preferred_element_type=F32)
                total += jnp.dot(alo[t, kk], bhi[q, kk], preferred_element_type=F32)
            prod[t, q] = total
            x_copy(t, q).start()

        for stage, lag in ((x_stage, lag_x), (z_stage, lag_z), (a_stage, lag_a + k)):
            @pl.when((v >= lag) & (v < steps + lag))
            def _(lag=lag):
                stage(v - lag, 0)
        return carry

    lax.fori_loop(0, steps + lag_a + 1, turn, 0)

    def write(q):
        return pltpu.make_async_copy(got.at[q], c_out.at[:, pl.ds(q * width, width)], out_s.at[q])

    diag = [jnp.zeros((tile, tile), F32) for _ in range(rows // tile)]
    for q in range(chunks):
        _, b1, b2 = order(t_of(2 * zl + xl), q)
        for u in range(2):
            for v in range(2):
                @pl.when(jnp.logical_not((u == b1) & (v == b2) & (xh == 0) & (k == 0)))
                def _():
                    spot = got.at[q, pl.ds(2 * part * u + part * v, part)]
                    copy(spot, spot, b_s.at[0, 0], b_r.at[q, u, v], other_core).wait_recv()
        cols = slice(q * width, (q + 1) * width)
        write(q).start()
        for t in range(len(diag)):
            span = slice(t * tile, (t + 1) * tile)
            hi, lo = split(got[q, span])
            for left, right in ((hi, lhi), (hi, llo), (lo, lhi)):
                diag[t] += lax.dot_general(left, right[span, cols], NT, preferred_element_type=F32)
    for t in range(len(diag)):
        dsend[:, :, t * tile:(t + 1) * tile] = diag[t].reshape(8, tile // 8, tile)

    def d_copy(d):
        to = (j + d) % 8
        return copy(dsend.at[to], dr.at[j], d_s.at[d], d_r.at[j], (me_r, half * 8 + to))

    def d_from(d):
        frm = (j + d) % 8
        return copy(dsend.at[frm], dr.at[frm], d_s.at[d], d_r.at[frm], (me_r, half * 8 + frm))

    for d in range(1, 8):
        d_copy(d).start()
    cross().wait_send()
    spread_end(l_ref, 0, l_s)
    spread_end(lx, 1, f_s)
    for t in (1, 2):
        onward(t).wait_send()
    for q in range(chunks):
        far_copy(q).wait_send()
        core_copy(k, q).wait_send()

    def sent(n, carry):
        t, q, dy = where_of(n)
        ys = (y + 4 - dy) % 4
        x_copy(t, q).wait_send()
        z_copy(t, q).wait_send()

        @pl.when(t > 0)
        def _():
            a_copy(t, q, dy).wait_send()

        @pl.when(jnp.logical_not(b_stays(ys)))
        def _():
            b_copy(ys, q).wait_send()
        return carry

    lax.fori_loop(0, steps, sent, 0)
    for q in range(chunks):
        write(q).wait()
    dr[j] = dsend[j]
    for d in range(1, 8):
        d_from(d).wait_recv()
    total = dr[0]
    for d in range(1, 8):
        total += dr[d]
    summed[...] = total

    stay_g = pltpu.make_async_copy(summed, g_out.at[me_c], g_r.at[me_c])

    def g_copy(d):
        return copy(summed, g_out.at[me_c], g_s.at[d], g_r.at[me_c], (me_r, (me_c + 2 * d) % 16))

    def g_from(d):
        frm = (me_c + 2 * d) % 16
        return copy(summed, g_out.at[frm], g_s.at[d], g_r.at[frm], (me_r, frm))

    def h_copy(d):
        frm = (me_c + 2 * d) % 16
        src = summed if d == 0 else g_out.at[frm]
        return copy(src, g_out.at[frm], g_s.at[8 + d], g_r.at[frm], other_core)

    def h_from(d):
        frm = (me_c + 1 - 2 * k + 2 * d) % 16
        return copy(summed, g_out.at[frm], g_s.at[8 + d], g_r.at[frm], other_core)

    for d in range(1, 8):
        g_copy(d).start()
    h_copy(0).start()
    stay_g.start()
    for d in range(1, 8):
        g_from(d).wait_recv()
        h_copy(d).start()
    for d in range(8):
        h_from(d).wait_recv()
    stay_g.wait()

    for d in range(1, 8):
        d_copy(d).wait_send()
    for d in range(1, 8):
        g_copy(d).wait_send()
    for d in range(8):
        h_copy(d).wait_send()


def finish(c_ref, g_ref, pd_ref, c_out, m_out):
    c_out[...] = c_ref[...]
    for h in range(2):
        m_out[:, h, :] = pd_ref[:, h, :] - g_ref[h]


def local(root_sigma, pivot_diag, update_l, update_map):
    tile = pivot_diag.shape[0]
    rows, cols = update_l.shape
    chunks, parts = 3, 2
    width = cols // chunks
    sem = pltpu.SemaphoreType.DMA
    vmem = pl.BlockSpec(memory_space=pltpu.VMEM)
    anywhere = pl.BlockSpec(memory_space=pl.ANY)
    product, diagonal = pl.pallas_call(
        kernel,
        out_shape=(jax.ShapeDtypeStruct(update_l.shape, F32), jax.ShapeDtypeStruct((16, tile // 8, rows), F32)),
        in_specs=[pl.BlockSpec(memory_space=pltpu.SMEM), anywhere, anywhere],
        out_specs=(anywhere, anywhere),
        scratch_shapes=[
            pltpu.VMEM((root_sigma.shape[0] // tile, tile, root_sigma.shape[1]), F32),
            pltpu.VMEM((rows, cols), F32),
            pltpu.VMEM((rows, cols), BF16),
            pltpu.VMEM((rows, cols), BF16),
            pltpu.VMEM((chunks, width, cols), F32),
            pltpu.VMEM((chunks, width, cols), F32),
            pltpu.VMEM((2, chunks, cols, width), F32),
            pltpu.VMEM((chunks, 2, cols, width), BF16),
            pltpu.VMEM((chunks, 2, cols, width), BF16),
            pltpu.VMEM((rows, cols), F32),
            pltpu.VMEM((4, 2, rows, cols), F32),
            pltpu.VMEM((4, 2, rows, cols), BF16),
            pltpu.VMEM((4, 2, rows, cols), BF16),
            pltpu.VMEM((4, chunks, rows, width), F32),
            pltpu.VMEM((4, chunks, rows // 2, width), F32),
            pltpu.VMEM((4, chunks, rows // 4, width), F32),
            pltpu.VMEM((4, chunks, rows // 4, width), F32),
            pltpu.VMEM((4, chunks, rows // 4, width), F32),
            pltpu.VMEM((chunks, rows, width), F32),
            pltpu.VMEM((8, tile // 8, rows), F32),
            pltpu.VMEM((8, tile // 8, rows), F32),
            pltpu.VMEM((tile // 8, rows), F32),
            sem((2,)), sem((chunks,)),
            sem((chunks,)), sem((chunks,)), sem((chunks,)), sem((chunks,)),
            sem, sem, sem((4,)), sem((4,)), sem((2,)), sem((4, 2)),
            sem((4, chunks)), sem((4, chunks)), sem((4, chunks)), sem((4, chunks)),
            sem((4, chunks)), sem((4, chunks)), sem((4, chunks)), sem((chunks, 2, 2)),
            sem((8,)), sem((8,)), sem((16,)), sem((16,)),
        ],
        compiler_params=pltpu.CompilerParams(
            collective_id=0, has_side_effects=True, vmem_limit_bytes=62 * 2**20),
        name="selected_inverse",
    )(update_map, root_sigma.reshape(-1, tile, root_sigma.shape[1]), update_l)
    return pl.pallas_call(
        finish,
        out_shape=(jax.ShapeDtypeStruct(update_l.shape, F32), jax.ShapeDtypeStruct(pivot_diag.shape, F32)),
        grid=(parts,),
        in_specs=[
            pl.BlockSpec((rows // parts, cols), lambda n: (n, 0)),
            pl.BlockSpec((2, tile // parts, rows), lambda n: (0, n, 0)),
            pl.BlockSpec((tile // parts, 2, rows), lambda n: (n, 0, 0)),
        ],
        out_specs=(
            pl.BlockSpec((rows // parts, cols), lambda n: (n, 0)),
            pl.BlockSpec((tile // parts, 2, rows), lambda n: (n, 0, 0)),
        ),
        name="write_results",
    )(product, diagonal.reshape(2, tile, rows), pivot_diag)


def solution(mesh):
    placed = (P("prow", "pcol"), P(None, None, "prow"), P("prow", "pcol"), P())
    return jax.shard_map(
        local,
        mesh=mesh,
        in_specs=placed,
        out_specs=(P("prow", "pcol"), P(None, None, "prow")),
        check_vma=False,
    )
```

```python
import jax
import jax.numpy as jnp
from jax import lax
from jax.experimental import pallas as pl
from jax.experimental.pallas import tpu as pltpu
from jax.sharding import PartitionSpec as P

MESH = pl.DeviceIdType.MESH
F32, BF16 = jnp.float32, jnp.bfloat16
NT = (((1,), (1,)), ((), ()))


def split(x):
    hi = x.astype(BF16)
    return hi, (x - hi.astype(F32)).astype(BF16)


def kernel(umap, sig_in, l_in, c_out, g_out, sig, l_ref, lhi, llo, fs, rc, stf, bhi, blo, lx, lb, ahi, alo, prod, xr, zr, fin, leg, got, dsend, dr, summed,
           in_s, out_s, zs_s, zs_r, cs_s, cs_r, lx_s, lx_r, l_s, f_s, o_s, l_r, x_s, x_r, z_s, z_r, a_s, a_r, b_s, b_r, d_s, d_r, g_s, g_r):
    me_r, me_c = lax.axis_index("prow"), lax.axis_index("pcol")
    y, xh = me_r // 2, me_r % 2
    half, j = me_c // 8, me_c % 8
    zl, xl, k = j // 4, (j // 2) % 2, j % 2
    chunks, width = fs.shape[0], fs.shape[1]
    tile = sig.shape[1]
    tiles = 2 * chunks
    rows = l_ref.shape[0]
    part = rows // 4
    steps = 4 * chunks

    def dev(y_, xh_, zl_, xl_, k_):
        return (y_ * 2 + xh_, half * 8 + zl_ * 4 + xl_ * 2 + k_)

    partner = (me_r, (me_c + 8) % 16)
    other_core = dev(y, xh, zl, xl, 1 - k)

    def copy(src, dst, ssem, rsem, to):
        return pltpu.make_async_remote_copy(
            src_ref=src, dst_ref=dst, send_sem=ssem, recv_sem=rsem, device_id=to, device_id_type=MESH)

    load_l = pltpu.make_async_copy(l_in, l_ref, in_s.at[0])
    load_sig = pltpu.make_async_copy(sig_in, sig, in_s.at[1])
    load_l.start()
    load_sig.start()

    barrier = pltpu.get_barrier_semaphore()

    def greet(to):
        pl.semaphore_signal(barrier, inc=1, device_id=to, device_id_type=MESH)

    greet(dev(y, 1 - xh, zl, xl, k))
    for d in (1, 3):
        for kk in range(2):
            greet(dev((y + d) % 4, xh, zl, xl, kk))
    greet(dev((y + 2) % 4, xh, zl, xl, k))
    for d in range(1, 8):
        greet((me_r, half * 8 + (j + d) % 8))
    for d in range(4):
        greet((me_r, (1 - half) * 8 + 2 * d + k))

    @pl.when(k == 1 - xh)
    def _():
        for d in range(4):
            greet((2 * y + 1 - xh, half * 8 + 2 * d + 1))

    load_sig.wait()
    for q in range(chunks):
        for h in range(2):
            row = umap[1 - half, me_r * tiles + 2 * q + h] // 8
            fs[q, h * tile:(h + 1) * tile, :] = sig[row]
    pl.semaphore_wait(barrier, 17 + 4 * k)

    def cross():
        return copy(l_ref, lx, lx_s, lx_r, dev(y, 1 - xh, zl, xl, k))

    def spread(src, core, sems, d):
        return copy(src, lb.at[y, k], sems.at[d], l_r.at[y, k], dev((y + d) % 4, xh, zl, xl, core))

    def spread_start(src, core, sems):
        for d in (1, 3):
            spread(src, core, sems, d).start()

        @pl.when(k != core)
        def _():
            spread(src, core, sems, 0).start()

        @pl.when(k == core)
        def _():
            pltpu.make_async_copy(src, lb.at[y, core], l_r.at[y, core]).start()

    def spread_end(src, core, sems):
        for d in (1, 3):
            spread(src, core, sems, d).wait_send()

        @pl.when(k != core)
        def _():
            spread(src, core, sems, 0).wait_send()

    def onward(t):
        yf, yt, kk = (y + 1 + 2 * (t - 1)) % 4, (y + 3 - 2 * (t - 1)) % 4, 2 - t
        return copy(lb.at[yf, kk], lb.at[yf, kk], o_s.at[t - 1], l_r.at[yf, kk], dev(yt, xh, zl, xl, k))

    load_l.wait()
    def arrived(yf, kk):
        copy(lb.at[yf, kk], lb.at[yf, kk], l_s.at[0], l_r.at[yf, kk], other_core).wait_recv()

    cross().start()
    spread_start(l_ref, 0, l_s)

    def far_copy(q):
        return copy(fs.at[q], rc.at[q], zs_s.at[q], zs_r.at[q], partner)

    for q in range(chunks):
        far_copy(q).start()
    hi, lo = split(l_ref[...])
    lhi[...] = hi
    llo[...] = lo

    def core_copy(kk, q):
        return copy(stf.at[kk, q], stf.at[kk, q], cs_s.at[q], cs_r.at[q], other_core)

    def take_s(q):
        far_copy(q).wait_recv()
        for h in range(2):
            row = umap[half, me_r * tiles + 2 * q + h] // 8
            near = sig[row]
            far = rc[q, h * tile:(h + 1) * tile, :]
            for s in range(tiles):
                col = umap[half, j * tiles + s]
                spot = col // 16 + tiles * (((col // 8) % 2 + half) % 2)
                x = near[:, :tile]
                for c in range(1, 2 * tiles):
                    lanes = slice((c % tiles) * tile, (c % tiles + 1) * tile)
                    x = jnp.where(spot == c, (near if c < tiles else far)[:, lanes], x)
                stf[k, q, s * tile:(s + 1) * tile, h * tile:(h + 1) * tile] = x.T
        core_copy(k, q).start()
        hi, lo = split(stf[k, q])
        bhi[q, k] = hi
        blo[q, k] = lo
        core_copy(1 - k, q).wait_recv()
        hi, lo = split(stf[1 - k, q])
        bhi[q, 1 - k] = hi
        blo[q, 1 - k] = lo

    def where_of(n):
        last = n // (3 * chunks)
        t = (1 - k) * ((1 - last) * (n % 3) + last * 3) + k * (n // chunks)
        q = (1 - k) * ((1 - last) * (n // 3) + last * (n - 3 * chunks)) + k * (n % chunks)
        return t, q, t + (t // 2) * (1 - 2 * (t % 2))

    def order(t, q):
        f = (q // (chunks - 1)) * (t // 2)
        return f, f * zl + (1 - f) * xl, f * xl + (1 - f) * zl

    def peer(f):
        return dev(y, xh, zl + f * (1 - 2 * zl), xl + (1 - f) * (1 - 2 * xl), k)

    def x_copy(t, q):
        f, b1, _ = order(t, q)
        return copy(prod.at[t, q, pl.ds(2 * part * (1 - b1), 2 * part)], xr.at[t, q], x_s.at[t, q], x_r.at[t, q], peer(f))

    def z_copy(t, q):
        f, _, b2 = order(t, q)
        return copy(xr.at[t, q, pl.ds(part * (1 - b2), part)], zr.at[t, q], z_s.at[t, q], z_r.at[t, q], peer(1 - f))

    def spot_of(t, q):
        _, b1, b2 = order(t, q)
        return pl.ds(2 * part * b1 + part * b2, part)

    def a_copy(t, q, dy):
        return copy(fin.at[t, q], leg.at[y, q], a_s.at[t, q], a_r.at[y, q], dev((y + dy) % 4, xh, zl, xl, k))

    def t_of(ys):
        dy = (y + 4 - ys) % 4
        return dy + (dy // 2) * (1 - 2 * (dy % 2))

    def b_copy(ys, q):
        t = t_of(ys)
        _, b1, b2 = order(t, q)
        to = dev(y, (xh + k) % 2, ys // 2, ys % 2, xh)
        return copy(leg.at[ys, q], got.at[q, spot_of(t, q)], b_s.at[ys, q], b_r.at[q, b1, b2], to)

    def b_stays(ys):
        return (ys == 2 * zl + xl) & (xh == 0) & (k == 0)

    lag_x, lag_z, lag_a = 2, 4, 8

    def x_stage(n, carry):
        t, q, _ = where_of(n)
        _, b1, b2 = order(t, q)
        x_copy(t, q).wait_recv()

        def add(b):
            at = pl.ds(part * b, part)
            xr[t, q, at] = xr[t, q, at] + prod[t, q, pl.ds(2 * part * b1 + part * b, part)]

        add(1 - b2)
        z_copy(t, q).start()
        add(b2)
        return carry

    def z_stage(n, carry):
        t, q, dy = where_of(n)
        _, _, b2 = order(t, q)
        z_copy(t, q).wait_recv()
        done = -(xr[t, q, pl.ds(part * b2, part)] + zr[t, q])

        @pl.when(t == 0)
        def _():
            leg[y, q] = done

        @pl.when(t > 0)
        def _():
            fin[t, q] = done
            a_copy(t, q, dy).start()
        return carry

    def a_stage(n, carry):
        t, q, dy = where_of(n)
        ys = (y + 4 - dy) % 4

        @pl.when(t > 0)
        def _():
            copy(leg.at[ys, q], leg.at[ys, q], a_s.at[0, 0], a_r.at[ys, q], other_core).wait_recv()

        @pl.when(b_stays(ys))
        def _():
            got[q, spot_of(t_of(ys), q)] = leg[ys, q]

        @pl.when(jnp.logical_not(b_stays(ys)))
        def _():
            b_copy(ys, q).start()
        return carry

    def turn(v, carry):
        @pl.when(v < steps)
        def _():
            n = v
            t, q, dy = where_of(n)
            yp = (y + dy) % 4

            @pl.when(t == 0)
            def _():
                take_s(q)

            @pl.when(n == 1 - k)
            def _():
                cross().wait_recv()
                spread_start(lx, 1, f_s)

            @pl.when(q == 0)
            def _():
                arrived(yp, 1)

                @pl.when(t != 2)
                def _():
                    arrived(yp, 0)

                @pl.when(t == 1)
                def _():
                    onward(1).start()
                    arrived((y + 3) % 4, 0)
                    onward(2).start()

                for kk in range(2):
                    hi, lo = split(lb[yp, kk])
                    ahi[t, kk] = hi
                    alo[t, kk] = lo

            total = jnp.zeros((rows, width), F32)
            for kk in range(2):
                total += jnp.dot(ahi[t, kk], bhi[q, kk], preferred_element_type=F32)
                total += jnp.dot(ahi[t, kk], blo[q, kk], preferred_element_type=F32)
                total += jnp.dot(alo[t, kk], bhi[q, kk], preferred_element_type=F32)
            prod[t, q] = total
            x_copy(t, q).start()

        for stage, lag in ((x_stage, lag_x), (z_stage, lag_z), (a_stage, lag_a + k)):
            @pl.when((v >= lag) & (v < steps + lag))
            def _(lag=lag):
                stage(v - lag, 0)
        return carry

    lax.fori_loop(0, steps + lag_a + 1, turn, 0)

    def write(q):
        return pltpu.make_async_copy(got.at[q], c_out.at[:, pl.ds(q * width, width)], out_s.at[q])

    diag = [jnp.zeros((tile, tile), F32) for _ in range(rows // tile)]
    for q in range(chunks):
        _, b1, b2 = order(t_of(2 * zl + xl), q)
        for u in range(2):
            for v in range(2):
                @pl.when(jnp.logical_not((u == b1) & (v == b2) & (xh == 0) & (k == 0)))
                def _():
                    spot = got.at[q, pl.ds(2 * part * u + part * v, part)]
                    copy(spot, spot, b_s.at[0, 0], b_r.at[q, u, v], other_core).wait_recv()
        cols = slice(q * width, (q + 1) * width)
        write(q).start()
        for t in range(len(diag)):
            span = slice(t * tile, (t + 1) * tile)
            hi, lo = split(got[q, span])
            for left, right in ((hi, lhi), (hi, llo), (lo, lhi)):
                diag[t] += lax.dot_general(left, right[span, cols], NT, preferred_element_type=F32)
    for t in range(len(diag)):
        dsend[:, :, t * tile:(t + 1) * tile] = diag[t].reshape(8, tile // 8, tile)

    def d_copy(d):
        to = (j + d) % 8
        return copy(dsend.at[to], dr.at[j], d_s.at[d], d_r.at[j], (me_r, half * 8 + to))

    def d_from(d):
        frm = (j + d) % 8
        return copy(dsend.at[frm], dr.at[frm], d_s.at[d], d_r.at[frm], (me_r, half * 8 + frm))

    for d in range(1, 8):
        d_copy(d).start()
    cross().wait_send()
    spread_end(l_ref, 0, l_s)
    spread_end(lx, 1, f_s)
    for t in (1, 2):
        onward(t).wait_send()
    for q in range(chunks):
        far_copy(q).wait_send()
        core_copy(k, q).wait_send()

    def sent(n, carry):
        t, q, dy = where_of(n)
        ys = (y + 4 - dy) % 4
        x_copy(t, q).wait_send()
        z_copy(t, q).wait_send()

        @pl.when(t > 0)
        def _():
            a_copy(t, q, dy).wait_send()

        @pl.when(jnp.logical_not(b_stays(ys)))
        def _():
            b_copy(ys, q).wait_send()
        return carry

    lax.fori_loop(0, steps, sent, 0)
    for q in range(chunks):
        write(q).wait()
    dr[j] = dsend[j]
    for d in range(1, 8):
        d_from(d).wait_recv()
    total = dr[0]
    for d in range(1, 8):
        total += dr[d]
    summed[...] = total

    stay_g = pltpu.make_async_copy(summed, g_out.at[me_c], g_r.at[me_c])

    def g_copy(d):
        return copy(summed, g_out.at[me_c], g_s.at[d], g_r.at[me_c], (me_r, (me_c + 2 * d) % 16))

    def g_from(d):
        frm = (me_c + 2 * d) % 16
        return copy(summed, g_out.at[frm], g_s.at[d], g_r.at[frm], (me_r, frm))

    def h_copy(d):
        frm = (me_c + 2 * d) % 16
        src = summed if d == 0 else g_out.at[frm]
        return copy(src, g_out.at[frm], g_s.at[8 + d], g_r.at[frm], other_core)

    def h_from(d):
        frm = (me_c + 1 - 2 * k + 2 * d) % 16
        return copy(summed, g_out.at[frm], g_s.at[8 + d], g_r.at[frm], other_core)

    for d in range(1, 8):
        g_copy(d).start()
    h_copy(0).start()
    stay_g.start()
    for d in range(1, 8):
        g_from(d).wait_recv()
        h_copy(d).start()
    for d in range(8):
        h_from(d).wait_recv()
    stay_g.wait()

    for d in range(1, 8):
        d_copy(d).wait_send()
    for d in range(1, 8):
        g_copy(d).wait_send()
    for d in range(8):
        h_copy(d).wait_send()


def finish(c_ref, g_ref, pd_ref, c_out, m_out):
    c_out[...] = c_ref[...]
    for h in range(2):
        m_out[:, h, :] = pd_ref[:, h, :] - g_ref[h]


def local(root_sigma, pivot_diag, update_l, update_map):
    tile = pivot_diag.shape[0]
    rows, cols = update_l.shape
    chunks, parts = 3, 2
    width = cols // chunks
    sem = pltpu.SemaphoreType.DMA
    vmem = pl.BlockSpec(memory_space=pltpu.VMEM)
    anywhere = pl.BlockSpec(memory_space=pl.ANY)
    product, diagonal = pl.pallas_call(
        kernel,
        out_shape=(jax.ShapeDtypeStruct(update_l.shape, F32), jax.ShapeDtypeStruct((16, tile // 8, rows), F32)),
        in_specs=[pl.BlockSpec(memory_space=pltpu.SMEM), anywhere, anywhere],
        out_specs=(anywhere, anywhere),
        scratch_shapes=[
            pltpu.VMEM((root_sigma.shape[0] // tile, tile, root_sigma.shape[1]), F32),
            pltpu.VMEM((rows, cols), F32),
            pltpu.VMEM((rows, cols), BF16),
            pltpu.VMEM((rows, cols), BF16),
            pltpu.VMEM((chunks, width, cols), F32),
            pltpu.VMEM((chunks, width, cols), F32),
            pltpu.VMEM((2, chunks, cols, width), F32),
            pltpu.VMEM((chunks, 2, cols, width), BF16),
            pltpu.VMEM((chunks, 2, cols, width), BF16),
            pltpu.VMEM((rows, cols), F32),
            pltpu.VMEM((4, 2, rows, cols), F32),
            pltpu.VMEM((4, 2, rows, cols), BF16),
            pltpu.VMEM((4, 2, rows, cols), BF16),
            pltpu.VMEM((4, chunks, rows, width), F32),
            pltpu.VMEM((4, chunks, rows // 2, width), F32),
            pltpu.VMEM((4, chunks, rows // 4, width), F32),
            pltpu.VMEM((4, chunks, rows // 4, width), F32),
            pltpu.VMEM((4, chunks, rows // 4, width), F32),
            pltpu.VMEM((chunks, rows, width), F32),
            pltpu.VMEM((8, tile // 8, rows), F32),
            pltpu.VMEM((8, tile // 8, rows), F32),
            pltpu.VMEM((tile // 8, rows), F32),
            sem((2,)), sem((chunks,)),
            sem((chunks,)), sem((chunks,)), sem((chunks,)), sem((chunks,)),
            sem, sem, sem((4,)), sem((4,)), sem((2,)), sem((4, 2)),
            sem((4, chunks)), sem((4, chunks)), sem((4, chunks)), sem((4, chunks)),
            sem((4, chunks)), sem((4, chunks)), sem((4, chunks)), sem((chunks, 2, 2)),
            sem((8,)), sem((8,)), sem((16,)), sem((16,)),
        ],
        compiler_params=pltpu.CompilerParams(
            collective_id=0, has_side_effects=True, vmem_limit_bytes=62 * 2**20),
        name="selected_inverse",
    )(update_map, root_sigma.reshape(-1, tile, root_sigma.shape[1]), update_l)
    return pl.pallas_call(
        finish,
        out_shape=(jax.ShapeDtypeStruct(update_l.shape, F32), jax.ShapeDtypeStruct(pivot_diag.shape, F32)),
        grid=(parts,),
        in_specs=[
            pl.BlockSpec((rows // parts, cols), lambda n: (n, 0)),
            pl.BlockSpec((2, tile // parts, rows), lambda n: (0, n, 0)),
            pl.BlockSpec((tile // parts, 2, rows), lambda n: (n, 0, 0)),
        ],
        out_specs=(
            pl.BlockSpec((rows // parts, cols), lambda n: (n, 0)),
            pl.BlockSpec((tile // parts, 2, rows), lambda n: (n, 0, 0)),
        ),
        name="write_results",
    )(product, diagonal.reshape(2, tile, rows), pivot_diag)


def solution(mesh):
    placed = (P("prow", "pcol"), P(None, None, "prow"), P("prow", "pcol"), P())
    return jax.shard_map(
        local,
        mesh=mesh,
        in_specs=placed,
        out_specs=(P("prow", "pcol"), P(None, None, "prow")),
        check_vma=False,
    )
```
